32 devices in a mesh: scen: 8 (over z, x), row: 4 (over y, core).
Axes of the slice: x: 2, y: 2, z: 4, core: 2. Of those that a mesh axis runs over, the one named last changes fastest.
Arguments:
- border: bfloat16 [128, 8192, 128], P('scen', 'row'), may hold values from -0.119628906 to 0.119628906
- col_index: int32 [128, 128], P('scen'), may hold values from 0 to 4095
- barrier: float32 [4096], replicated, may hold values from 0.3 to 3
- counts: int32 [8], replicated, may hold values from 1 to 16, as said below
- inverse: bfloat16 [1024, 1024], replicated, may hold values from -0.140625 to 0.140625
- slab: float32 [8192, 4096], P('row', 'scen'), may hold values from -1.5 to 1.5
Outputs:
- updated: float32 [8192, 4096], P('row', 'scen')
The draws below stay inside these ranges and needn't reach their ends.
Inputs may be any that keep to these rules, and one draw needn't show every extreme that they name: `counts`: the scenario groups whose index differs by a multiple of 4 from one drawn index hold 16 live blocks; every other group holds 1 to 4.
All inputs are finite; a program needn't handle non-finite values.
Results may differ from the reference program's by a relative error of at most 0.0064.
Values may be sent and summed in bfloat16 or wider, within the bound.
No kernel may reach another device: no remote copies, remote signals or barrier semaphores. Data moves between devices by JAX's collectives and lax.ppermute only.
A program may use at most 128 MiB of HBM per device.

```python
import math
import jax
import jax.numpy as jnp
from jax import lax

NF = 8192
PW = 1024
NT = 4096
BW = 128
NCOL = 4096
SLOTS = 16
BLOCKS = 128
N_SCEN = 8
N_ROW = 4


def draw_counts(key, part):
    first_key, second_key = jax.random.split(jax.random.fold_in(key, 11))
    shift_value = jax.random.randint(first_key, (), 0, N_SCEN, dtype=jnp.int32)
    group_ids = jnp.arange(N_SCEN, dtype=jnp.int32)
    light_counts = jax.random.randint(second_key, (N_SCEN,), 1, SLOTS // 4 + 1, dtype=jnp.int32)
    crowded = (group_ids - shift_value) % 4 == 0
    return jnp.where(crowded, SLOTS, light_counts).astype(jnp.int32)


def place_ends(values, stream_key, smallest, largest):
    shape = values.shape
    place = [jax.random.randint(jax.random.fold_in(stream_key, axis), (), 0, shape[axis]) for axis in range(len(shape))]
    values = values.at[tuple(place)].set(smallest)
    longest = shape.index(max(shape))
    place[longest] = (place[longest] + 1) % shape[longest]
    return values.at[tuple(place)].set(largest)


def block_scale(key, dims, cuts, low, high):
    gain, own = 1.0, jax.random.fold_in(key, 6)
    for position, parts in cuts:
        steps = jnp.exp(jax.random.uniform(jax.random.fold_in(own, position), (parts,), jnp.float32, low / len(cuts), high / len(cuts)))
        gain = gain * jnp.repeat(steps, dims[position] // parts).reshape([-1 if axis == position else 1 for axis in range(len(dims))])
    return gain


def scatter_about(stream_key, extent, width, bound, cuts=(), kind=jnp.bfloat16):
    level = block_scale(stream_key, extent, cuts, -0.22, 0.18) if cuts else 1.0
    entries = jax.random.normal(stream_key, extent, jnp.float32) * width * level
    return jnp.minimum(jnp.maximum(entries, -bound), bound).astype(kind)


def setup_inputs(seed: int = 0) -> dict:
    streams_of = jax.random.split(jax.random.key(seed), 7)
    return {
        "border": scatter_about(streams_of[0], (BLOCKS, NF, BW), 0.02, 0.119628906, ((0, 8), (1, 4))),
        "col_index": place_ends(jax.random.randint(streams_of[1], (BLOCKS, BW), 0, NCOL), jax.random.fold_in(streams_of[1], 1), 0, NCOL - 1).astype(jnp.int32),
        "barrier": jnp.clip(jnp.exp(jax.random.uniform(streams_of[2], (NCOL,), jnp.float32, math.log(0.3), math.log(3.0))), 0.3, 3.0),
        "counts": draw_counts(jax.random.fold_in(streams_of[6], 71), 0),
        "inverse": scatter_about(streams_of[4], (PW, PW), (24.0 / PW), 0.140625),
        "slab": scatter_about(streams_of[5], (NF, NT), 0.25, 1.5, ((0, 4), (1, 8)), jnp.float32),
    }


def reference(border, col_index, barrier, counts, inverse, slab):
    share_width = PW // N_ROW
    local_rows = NF // N_ROW
    columns = jnp.arange(PW, dtype=jnp.int32)
    panel_vars = ((columns // share_width) * local_rows + columns % share_width).astype(jnp.int32)
    block_ids = jnp.arange(N_SCEN * SLOTS, dtype=jnp.int32)

    def accumulate(total, number):
        group = number // SLOTS
        within = number % SLOTS
        is_live = within < counts[group]

        def add_block(running):
            block = lax.dynamic_index_in_dim(border, number, 0, keepdims=False)
            indices = lax.dynamic_index_in_dim(col_index, number, 0, keepdims=False)
            weights = barrier[indices]
            scaled = (block.astype(jnp.float32) * weights[None, :]).astype(jnp.bfloat16)
            heads = scaled[panel_vars]
            return running + jnp.dot(scaled, heads.T, preferred_element_type=jnp.float32)

        def keep_block(running):
            return running

        return lax.cond(is_live, add_block, keep_block, total), None

    panel, unused = lax.scan(accumulate, jnp.zeros((NF, PW), jnp.float32), block_ids)
    rounded = panel.astype(jnp.bfloat16)
    finished = jnp.dot(rounded, inverse, preferred_element_type=jnp.float32).astype(jnp.bfloat16)
    trailing = rounded[:NT]
    return slab - jnp.dot(finished, trailing.T, preferred_element_type=jnp.float32)
```

```python
import functools

import jax
import jax.numpy as jnp
from jax import lax
from jax.experimental import pallas as pl
from jax.experimental.pallas import tpu as pltpu
from jax.sharding import PartitionSpec as P

f32, bf16 = jnp.float32, jnp.bfloat16
LANES = 128


def nt_dot(a, b):
    return lax.dot_general(a, b, (((1,), (1,)), ((), ())), preferred_element_type=f32)


def weights_kernel(place_ref, counts_ref, index_ref, table_ref, out_ref):
    index = index_ref[...]
    high, low = index // LANES, index % LANES
    total = jnp.zeros(index.shape, f32)
    for row in range(table_ref.shape[0]):
        entries = jnp.broadcast_to(table_ref[row : row + 1, :], index.shape)
        picked = jnp.take_along_axis(entries, low, axis=1, mode="promise_in_bounds")
        total = jnp.where(high == row, picked, total)
    live = lax.broadcasted_iota(jnp.int32, index.shape, 0) < counts_ref[place_ref[0]]
    out_ref[...] = jnp.where(live, total, 0.0)


def live_weights(place, counts, col_index, barrier):
    smem = pl.BlockSpec(memory_space=pltpu.SMEM)
    vmem = pl.BlockSpec(memory_space=pltpu.VMEM)
    return pl.pallas_call(
        weights_kernel,
        out_shape=jax.ShapeDtypeStruct(col_index.shape, f32),
        in_specs=[smem, smem, vmem, vmem],
        out_specs=vmem,
        name="live_weights",
    )(place, counts, col_index, barrier.reshape(-1, LANES))


def scaled_flat(blocks, weights):
    parts = [
        (blocks[k].astype(f32) * weights[k : k + 1, :]).astype(bf16) for k in range(blocks.shape[0])
    ]
    return jnp.concatenate(parts, axis=1)


def partial_kernel(order_ref, border_ref, heads_ref, weights_ref, *rest):
    outs, scaled_heads = rest[:-1], rest[-1]

    @pl.when(pl.program_id(0) == 0)
    def _():
        scaled_heads[...] = scaled_flat(heads_ref, weights_ref[...])

    value = nt_dot(scaled_flat(border_ref, weights_ref[...]), scaled_heads[...])
    for out in outs:
        out[...] = value.astype(out.dtype)


def partial_panel(order, position, border, heads, head_rows, weights, kinds):
    slots, rows, width = border.shape
    quarter = rows // 4
    steps = 2 if quarter % 512 == 0 else 1
    tile = quarter // steps
    return pl.pallas_call(
        partial_kernel,
        grid_spec=pltpu.PrefetchScalarGridSpec(
            num_scalar_prefetch=1,
            grid=(steps,),
            in_specs=[
                pl.BlockSpec((slots, tile, width), lambda i, o: (0, o[position] * steps + i, 0)),
                pl.BlockSpec((slots, head_rows, width), lambda i, o: (0, 0, 0)),
                pl.BlockSpec((slots, width), lambda i, o: (0, 0)),
            ],
            out_specs=[pl.BlockSpec((tile, head_rows), lambda i, o: (i, 0)) for _ in kinds],
            scratch_shapes=[pltpu.VMEM((head_rows, slots * width), bf16)],
        ),
        out_shape=[jax.ShapeDtypeStruct((quarter, head_rows), kind) for kind in kinds],
        compiler_params=pltpu.CompilerParams(vmem_limit_bytes=24 << 20),
        cost_estimate=pl.CostEstimate(
            flops=2 * quarter * head_rows * slots * width,
            bytes_accessed=2 * slots * (quarter + head_rows) * width,
            transcendentals=0,
        ),
        name="partial_panel",
    )(order, border, heads, weights)


def update_kernel(n, order_ref, inverse_ref, slab_ref, *rest):
    trailing, pieces, out_ref, w_ref = rest[:n], rest[n : 5 * n], rest[-2], rest[-1]
    position = pl.program_id(0)
    ends = [0]
    for t in trailing:
        ends.append(ends[-1] + t.shape[1])

    @pl.when(position == 0)
    def _():
        total = None
        for j in range(n):
            part = nt_dot(inverse_ref[:, ends[j] : ends[j + 1]], trailing[j][...])
            total = part if total is None else total + part
        w_ref[...] = total.astype(bf16)

    for p in range(4):

        @pl.when(position == p)
        def _(p=p):
            total = slab_ref[...]
            for j in range(n):
                total -= jnp.dot(
                    pieces[j * 4 + p][...],
                    w_ref[ends[j] : ends[j + 1], :],
                    preferred_element_type=f32,
                )
            out_ref[...] = total


def update(order, inverse, slab, trailing, pieces):
    rows, columns = slab.shape
    quarter = rows // 4
    n = len(trailing)
    flat = [piece for chunk in pieces for piece in chunk]
    whole = lambda a: pl.BlockSpec(a.shape, lambda i, o: (0, 0))
    block = pl.BlockSpec((quarter, columns), lambda i, o: (o[i], 0))
    return pl.pallas_call(
        functools.partial(update_kernel, n),
        grid_spec=pltpu.PrefetchScalarGridSpec(
            num_scalar_prefetch=1,
            grid=(4,),
            in_specs=[whole(inverse), block] + [whole(a) for a in trailing + flat],
            out_specs=block,
            scratch_shapes=[pltpu.VMEM((inverse.shape[0], columns), bf16)],
        ),
        out_shape=jax.ShapeDtypeStruct(slab.shape, slab.dtype),
        compiler_params=pltpu.CompilerParams(vmem_limit_bytes=40 << 20),
        name="update",
    )(order, inverse, slab, *trailing, *flat)


def body(border, col_index, barrier, counts, inverse, slab):
    scen_count, row_count = lax.axis_size("scen"), lax.axis_size("row")
    s, r = lax.axis_index("scen"), lax.axis_index("row")
    slots, local_rows, width = border.shape
    panel_width = inverse.shape[0]
    share = panel_width // row_count
    quarter = local_rows // 4
    trail = slab.shape[1]
    line = scen_count // 2
    half = line // 2
    x, z = s % 2, s // 2
    side = (z >= half).astype(jnp.int32)
    order = jnp.stack([x, 1 - x, 2 + side, 3 - side]).astype(jnp.int32)

    swap_x = [(i, i ^ 1) for i in range(scen_count)]
    at = lambda place, lane: place * 2 + lane

    def both_ends(a, b):
        pairs = []
        for lane in range(2):
            pairs += [(at(a, lane), at(b, lane)), (at(line - 1 - a, lane), at(line - 1 - b, lane))]
        return pairs

    inward = [both_ends(t, t + 1) for t in range(half - 1)]
    outward = [both_ends(t + 1, t) for t in reversed(range(half - 1))]
    middle = both_ends(half - 1, half)
    inner_x = [(i, i ^ 1) for i in (at(a, lane) for a in (half - 1, half) for lane in range(2))]
    spread_to = [(z == t) | (z == line - 1 - t) for t in reversed(range(half - 1))]
    over_scen = lambda value, pairs: lax.ppermute(value.astype(bf16), "scen", pairs)
    over_row = lambda value, mask: lax.ppermute(
        value, "row", [(i, i ^ mask) for i in range(row_count)]
    )

    own = border[:, :share, :]
    sibling = over_row(own, 1)
    far = [over_row(own, mask) for mask in range(2, row_count, 2)]
    far_sibling = [over_row(value, 1) for value in far]
    heads = [(border, share), (sibling, share)]
    if far:
        for group in (far, far_sibling):
            joined = group[0] if len(group) == 1 else jnp.concatenate(group, axis=1)
            heads.append((joined, joined.shape[1]))
    n = len(heads)

    def share_order(device):
        masks = [0, 1] + list(range(2, row_count, 2)) + list(range(3, row_count, 2))
        return [device ^ mask for mask in masks]

    first_row = s * trail
    source = first_row // local_rows

    def take(value, shares, axis):
        return jnp.concatenate(
            [lax.dynamic_slice_in_dim(value, k * share, share, axis) for k in shares], axis
        )

    inverse_here = take(take(inverse, share_order(r), 0), share_order(source), 1)
    weights = live_weights(s.astype(jnp.int32).reshape(1), counts, col_index, barrier)

    kinds = ([f32], [bf16], [f32, bf16], [f32, bf16])
    pieces, trailing = [], []
    unit = min(trail, quarter)

    for values, head_rows in heads:
        (send,) = partial_panel(order, 1, border, values, head_rows, weights, kinds[1])
        got = over_scen(send, swap_x)
        keep2, send2 = partial_panel(order, 2, border, values, head_rows, weights, kinds[2])
        keep3, send3 = partial_panel(order, 3, border, values, head_rows, weights, kinds[3])
        (keep,) = partial_panel(order, 0, border, values, head_rows, weights, kinds[0])
        total = keep + got.astype(f32)
        for pairs in inward:
            total = total + over_scen(total, pairs).astype(f32)
        total = total + over_scen(total, middle).astype(f32)
        final = total.astype(bf16)
        for pairs, mine in zip(outward, spread_to):
            final = jnp.where(mine, over_scen(final, pairs), final)
        other = over_scen(final, swap_x)
        for step, pairs in enumerate(inward):
            got2, got3 = over_scen(send2, pairs), over_scen(send3, pairs)
            keep2, keep3 = keep2 + got2.astype(f32), keep3 + got3.astype(f32)
            send2, send3 = keep2.astype(bf16), keep3.astype(bf16)
        keep2 = keep2 + over_scen(send3, middle).astype(f32)
        keep2 = keep2 + over_scen(keep2, inner_x).astype(f32)
        final2 = keep2.astype(bf16)
        final3 = over_scen(final2, middle)
        for pairs, mine in zip(outward, spread_to):
            got2, got3 = over_scen(final2, pairs), over_scen(final3, pairs)
            final2, final3 = jnp.where(mine, got2, final2), jnp.where(mine, got3, final3)
        chunk = [final, other, final2, final3]
        pieces.append(chunk)

        joined = jnp.concatenate(chunk, axis=0)
        parts = []
        for k in range(trail // unit):
            start = first_row % local_rows + k * unit
            place = start // quarter
            position = jnp.argmax(order == place).astype(jnp.int32)
            parts.append(
                lax.dynamic_slice_in_dim(joined, position * quarter + start % quarter, unit, 0)
            )
        rows = parts[0] if len(parts) == 1 else jnp.concatenate(parts, axis=0)
        rows = jnp.where(source == r, rows, jnp.zeros_like(rows))
        masks = []
        mask = row_count // 2
        while mask:
            masks.append(mask)
            mask //= 2
        reached = {g: {g * trail // local_rows} for g in range(scen_count)}
        for mask in masks:
            pairs = [
                (g * row_count + k, g * row_count + (k ^ mask))
                for g in range(scen_count)
                for k in sorted(reached[g])
            ]
            rows = rows + lax.ppermute(rows, ("scen", "row"), pairs)
            for g in range(scen_count):
                reached[g] |= {k ^ mask for k in reached[g]}
        trailing.append(rows)

    return update(order, inverse_here, slab, trailing, pieces)


def solution(mesh):
    return jax.shard_map(
        body,
        mesh=mesh,
        in_specs=(P("scen", "row", None), P("scen", None), P(), P(), P(), P("row", "scen")),
        out_specs=P("row", "scen"),
        check_vma=False,
    )
```

```python
import functools

import jax
import jax.numpy as jnp
from jax import lax
from jax.experimental import pallas as pl
from jax.experimental.pallas import tpu as pltpu
from jax.sharding import PartitionSpec as P

f32, bf16 = jnp.float32, jnp.bfloat16
LANES = 128
MIB = 1 << 20
LIMIT = 10 * MIB
IN_VMEM = pl.BlockSpec(memory_space=pltpu.VMEM)
IN_HBM = pl.BlockSpec(memory_space=pltpu.HBM)
PIECES = ((2, 3, 3), (4, 4))
UNIT, HOP, STEP, LEAD, FAR, SLAB = 2.85, 2.0, 1.5, 1.5, 20.0, 60.0
BATCHES = ((0, 1, 2), (3,))


def nt_dot(a, b):
    return lax.dot_general(a, b, (((1,), (1,)), ((), ())), preferred_element_type=f32)


def scaled_flat(blocks, weights):
    parts = [
        (blocks[k].astype(f32) * weights[k : k + 1, :]).astype(bf16) for k in range(blocks.shape[0])
    ]
    return jnp.concatenate(parts, axis=1)


def first_kernel(
    parts, place_ref, counts_ref, order_ref, index_ref, table_ref, border_ref, *rest
):
    weights_ref, heads_ref, scaled_ref, send_ref, held_heads, held, sems = rest
    slots, quarter, width = held.shape
    share = heads_ref.shape[0]
    step = slots // parts
    first = pl.multiple_of(order_ref[1] * quarter, quarter)
    near = pltpu.make_async_copy(border_ref.at[:, pl.ds(0, share), :], held_heads, sems.at[parts])
    near.start()
    copies = [
        pltpu.make_async_copy(
            border_ref.at[pl.ds(i * step, step), pl.ds(first, quarter), :],
            held.at[pl.ds(i * step, step)],
            sems.at[i],
        )
        for i in range(parts)
    ]
    for copy in copies:
        copy.start()

    index = index_ref[...]
    high, low = index // LANES, index % LANES
    total = jnp.zeros(index.shape, f32)
    for row in range(table_ref.shape[0]):
        entries = jnp.broadcast_to(table_ref[row : row + 1, :], index.shape)
        picked = jnp.take_along_axis(entries, low, axis=1, mode="promise_in_bounds")
        total = jnp.where(high == row, picked, total)
    live = lax.broadcasted_iota(jnp.int32, index.shape, 0) < counts_ref[place_ref[0]]
    weights_ref[...] = jnp.where(live, total, 0.0)

    near.wait()
    heads_ref[...] = scaled_flat(held_heads, weights_ref[...])
    for i, copy in enumerate(copies):
        copy.wait()
        scaled_ref[:, i * step * width : (i + 1) * step * width] = scaled_flat(
            held.at[pl.ds(i * step, step)], weights_ref[i * step : (i + 1) * step, :]
        )
    send_ref[...] = nt_dot(scaled_ref[...], heads_ref[...]).astype(bf16)


def first_step(place, counts, order, col_index, barrier, border, share):
    slots, rows, width = border.shape
    quarter = rows // 4
    parts = 4 if slots % 4 == 0 else 1
    smem = pl.BlockSpec(memory_space=pltpu.SMEM)
    whole = lambda shape: pl.BlockSpec(shape, lambda i: (0,) * len(shape))
    table = barrier.reshape(-1, LANES)
    shapes = [
        jax.ShapeDtypeStruct(col_index.shape, f32),
        jax.ShapeDtypeStruct((share, slots * width), bf16),
        jax.ShapeDtypeStruct((quarter, slots * width), bf16),
        jax.ShapeDtypeStruct((quarter, share), bf16),
    ]
    return pl.pallas_call(
        functools.partial(first_kernel, parts),
        grid=(1,),
        in_specs=[smem, smem, smem, whole(col_index.shape), whole(table.shape), IN_HBM],
        out_specs=[whole(out.shape) for out in shapes],
        out_shape=shapes,
        scratch_shapes=[
            pltpu.VMEM((slots, share, width), bf16),
            pltpu.VMEM((slots, quarter, width), bf16),
            pltpu.SemaphoreType.DMA((parts + 1,)),
        ],
        compiler_params=pltpu.CompilerParams(vmem_limit_bytes=58 * MIB),
        name="first_step",
    )(place, counts, order, col_index, table, border)


def scale_kernel(position, parts, order_ref, border_ref, weights_ref, out_ref, held, sems):
    slots, rows, width = held.shape
    first = pl.multiple_of(order_ref[position] * rows, rows)
    step = slots // parts
    copies = [
        pltpu.make_async_copy(
            border_ref.at[pl.ds(i * step, step), pl.ds(first, rows), :],
            held.at[pl.ds(i * step, step)],
            sems.at[i],
        )
        for i in range(parts)
    ]
    for copy in copies:
        copy.start()
    for i, copy in enumerate(copies):
        copy.wait()
        out_ref[:, i * step * width : (i + 1) * step * width] = scaled_flat(
            held.at[pl.ds(i * step, step)], weights_ref[i * step : (i + 1) * step, :]
        )


def scaled_quarter(order, position, border, weights):
    slots, rows, width = border.shape
    quarter = rows // 4
    parts = 4 if slots % 4 == 0 else 1
    return pl.pallas_call(
        functools.partial(scale_kernel, position, parts),
        in_specs=[pl.BlockSpec(memory_space=pltpu.SMEM), IN_HBM, IN_VMEM],
        out_specs=IN_VMEM,
        out_shape=jax.ShapeDtypeStruct((quarter, slots * width), bf16),
        scratch_shapes=[
            pltpu.VMEM((slots, quarter, width), bf16),
            pltpu.SemaphoreType.DMA((parts,)),
        ],
        compiler_params=pltpu.CompilerParams(vmem_limit_bytes=LIMIT),
        name="scaled_quarter",
    )(order, border, weights)


def piece_kernel(runs, adds, *refs):
    rows_refs, heads_refs = refs[:2], refs[2 : 2 + len({g for g, _, _, _ in runs})]
    rest = refs[2 + len(heads_refs) :]
    got, outs = rest[:adds], rest[adds:]
    groups = sorted({g for g, _, _, _ in runs})
    at = 0
    for g, half, begin, end in runs:
        value = nt_dot(rows_refs[half][begin:end, :], heads_refs[groups.index(g)][...])
        place = slice(at, at + end - begin)
        if adds:
            value += got[0][place, :].astype(f32)
        for out in outs:
            out[place, :] = value.astype(out.dtype)
        at += end - begin


def panel_piece(runs, scaled, heads, got, kinds):
    groups = sorted({g for g, _, _, _ in runs})
    rows = sum(end - begin for _, _, begin, end in runs)
    operands = [*scaled, *(heads[g] for g in groups), *got]
    return pl.pallas_call(
        functools.partial(piece_kernel, runs, len(got)),
        in_specs=[IN_VMEM] * len(operands),
        out_specs=[IN_VMEM] * len(kinds),
        out_shape=[jax.ShapeDtypeStruct((rows, heads[groups[0]].shape[0]), kind) for kind in kinds],
        compiler_params=pltpu.CompilerParams(vmem_limit_bytes=LIMIT),
        name="panel_piece",
    )(*operands)


def hold_kernel(order_ref, slab_ref, out_ref, sems):
    quarter = out_ref.shape[1]
    copies = []
    for p in range(4):
        rows = pl.ds(pl.multiple_of(order_ref[p] * quarter, quarter), quarter)
        copies.append(pltpu.make_async_copy(slab_ref.at[rows], out_ref.at[p], sems.at[p]))
    for copy in copies:
        copy.start()
    for copy in copies:
        copy.wait()


def held_slab(order, slab):
    rows, columns = slab.shape
    return pl.pallas_call(
        hold_kernel,
        in_specs=[pl.BlockSpec(memory_space=pltpu.SMEM), IN_HBM],
        out_specs=IN_VMEM,
        out_shape=jax.ShapeDtypeStruct((4, rows // 4, columns), slab.dtype),
        scratch_shapes=[pltpu.SemaphoreType.DMA((4,))],
        compiler_params=pltpu.CompilerParams(vmem_limit_bytes=LIMIT),
        name="held_slab",
    )(order, slab)


def factor_kernel(plan, ids_ref, inverse_ref, *rest):
    widths, sources = plan
    n = len(widths)
    trailing, rest = rest[: len(sources)], rest[len(sources) :]
    total_ref, out_ref = rest if len(rest) == 2 else (None, rest[0])
    ends = [sum(widths[:g]) for g in range(n + 1)]
    begin_of = lambda which, g: (
        ends[g] if ids_ref is None else pl.multiple_of(ids_ref[which, g] * widths[g], widths[g])
    )
    for g in range(n):
        total = None if total_ref is None else total_ref[ends[g] : ends[g + 1], :]
        for batch, groups in enumerate(sources):
            begin = 0
            for j in groups:
                block = inverse_ref[pl.ds(begin_of(0, g), widths[g]), pl.ds(begin_of(1, j), widths[j])]
                part = nt_dot(block, trailing[batch][:, begin : begin + widths[j]])
                total = part if total is None else total + part
                begin += widths[j]
        out_ref[ends[g] : ends[g + 1], :] = total.astype(out_ref.dtype)


def factor(ids, inverse, widths, sources, trailing, total, kind):
    smem = pl.BlockSpec(memory_space=pltpu.SMEM)

    def kernel(*refs):
        factor_kernel((widths, sources), *((None, *refs) if ids is None else refs))

    operands = ([] if ids is None else [ids]) + [inverse, *trailing, *total]
    return pl.pallas_call(
        kernel,
        in_specs=([] if ids is None else [smem]) + [IN_VMEM] * (1 + len(trailing) + len(total)),
        out_specs=IN_VMEM,
        out_shape=jax.ShapeDtypeStruct((inverse.shape[0], trailing[0].shape[0]), kind),
        compiler_params=pltpu.CompilerParams(vmem_limit_bytes=LIMIT),
        name="factor",
    )(*operands)


def update_kernel(plan, order_ref, slab_ref, factor_ref, *rest):
    widths, places = plan
    *pieces, out_ref, held, sems = rest
    quarter = held.shape[1]
    ends = [sum(widths[:g]) for g in range(len(widths) + 1)]
    stores = []
    for p in range(4):
        rows = pl.ds(pl.multiple_of(order_ref[p] * quarter, quarter), quarter)
        stores.append(pltpu.make_async_copy(held.at[p], out_ref.at[rows], sems.at[p]))
    for p in range(4):
        held[p] = slab_ref[p]
        for g, side, half, begin, end, piece, at in places:
            if 2 * half + side == p:
                held[p, begin:end, :] -= jnp.dot(
                    pieces[piece][at : at + end - begin, :],
                    factor_ref[ends[g] : ends[g + 1], :],
                    preferred_element_type=f32,
                )
        stores[p].start()
    for store in stores:
        store.wait()


def update(order, held, factor_value, plan, pieces):
    _, quarter, columns = held.shape
    return pl.pallas_call(
        functools.partial(update_kernel, plan),
        in_specs=[pl.BlockSpec(memory_space=pltpu.SMEM)] + [IN_VMEM] * (2 + len(pieces)),
        out_specs=IN_HBM,
        out_shape=jax.ShapeDtypeStruct((4 * quarter, columns), held.dtype),
        scratch_shapes=[
            pltpu.VMEM(held.shape, f32),
            pltpu.SemaphoreType.DMA((4,)),
        ],
        compiler_params=pltpu.CompilerParams(vmem_limit_bytes=LIMIT),
        name="update",
    )(order, held, factor_value, *pieces)


def body(border, col_index, barrier, counts, inverse, slab):
    scen_count, row_count = lax.axis_size("scen"), lax.axis_size("row")
    s, r = lax.axis_index("scen"), lax.axis_index("row")
    slots, local_rows, width = border.shape
    panel_width = inverse.shape[0]
    share = panel_width // row_count
    quarter = local_rows // 4
    trail = slab.shape[1]
    line = scen_count // 2
    half = line // 2
    x, z = s % 2, s // 2
    order = jnp.stack([x, 1 - x, 2 + x, 3 - x]).astype(jnp.int32)

    swap_x = [(i, i ^ 1) for i in range(scen_count)]
    at = lambda place, lane: place * 2 + lane

    def both_ends(a, b):
        pairs = []
        for lane in range(2):
            pairs += [(at(a, lane), at(b, lane)), (at(line - 1 - a, lane), at(line - 1 - b, lane))]
        return pairs

    inward = [both_ends(t, t + 1) for t in range(half - 1)]
    outward = [both_ends(t + 1, t) for t in reversed(range(half - 1))]
    middle = both_ends(half - 1, half)
    spread_to = [(z == t) | (z == line - 1 - t) for t in reversed(range(half - 1))]
    hops = len(inward)
    over_scen = lambda value, pairs: lax.ppermute(value.astype(bf16), "scen", pairs)
    over_row = lambda value, mask: lax.ppermute(
        value, "row", [(i, i ^ mask) for i in range(row_count)]
    )

    last = []

    def after(*values):
        if not last:
            return values if len(values) > 1 else values[0]
        out = lax.optimization_barrier((*values, *last))
        return out[: len(values)] if len(values) > 1 else out[0]

    def done(*values):
        last[:] = values

    place = s.astype(jnp.int32).reshape(1)
    weights, own, scaled_sent, first_send = first_step(
        place, counts, order, col_index, barrier, border, share
    )
    scaled = {1: scaled_sent}
    done(own)
    far = [over_row(own, mask) for mask in range(2, row_count, 2)]
    sibling = over_row(own, 1)
    joined = lambda group: group[0] if len(group) == 1 else jnp.concatenate(group, axis=0)
    heads = [own, sibling, None, None]
    widths = [share, share, share * len(far), share * len(far)]

    def share_order(device):
        masks = [0, 1] + list(range(2, row_count, 2)) + list(range(3, row_count, 2))
        return [device ^ mask for mask in masks]

    first_row = s * trail
    source = first_row // local_rows

    def take(value, shares, axis):
        return jnp.concatenate(
            [lax.dynamic_slice_in_dim(value, k * share, share, axis) for k in shares], axis
        )

    aligned = trail <= quarter and all(
        (g * trail) % local_rows // quarter % 2 == g % 2 for g in range(scen_count)
    )
    unit = min(trail, quarter)
    masks = [1 << k for k in reversed(range((row_count - 1).bit_length()))]
    spread = []
    reached = {g: {g * trail // local_rows} for g in range(scen_count)}
    for mask in masks:
        spread.append(
            [
                (g * row_count + k, g * row_count + (k ^ mask))
                for g in range(scen_count)
                for k in sorted(reached[g])
            ]
        )
        for g in range(scen_count):
            reached[g] |= {k ^ mask for k in reached[g]}

    eighth = quarter // 2
    pieces = []
    for pair, sizes in enumerate(PIECES):
        units = [(2 * pair + g, b // 2, b % 2) for g in range(2) for b in range(4)]
        for size in sizes:
            runs = []
            for g, half, part in units[:size]:
                if runs and runs[-1][:2] == (g, half):
                    runs[-1] = (*runs[-1][:3], (part + 1) * eighth)
                else:
                    runs.append((g, half, part * eighth, (part + 1) * eighth))
            pieces.append(runs)
            units = units[size:]
    sizes = [size for pair in PIECES for size in pair]
    count = len(pieces)
    offsets = []
    for runs in pieces:
        places, at_row = [], 0
        for g, h, begin, end in runs:
            places.append((g, h, begin, end, at_row))
            at_row += end - begin
        offsets.append(places)
    last_of = [max(k for k, runs in enumerate(pieces) if any(run[0] == g for run in runs)) for g in range(4)]

    def kept_rows(values, g):
        parts = []
        for k, places in enumerate(offsets):
            parts += [values[k][at : at + end - begin] for h, _, begin, end, at in places if h == g]
        return jnp.concatenate(parts, axis=0)

    def trailing_rows(groups):
        columns = []
        for g in groups:
            kept, parts = kept_rows(mine, g), []
            other = None if aligned else kept_rows(others, g)
            for i in range(trail // unit):
                start = first_row % local_rows + i * unit
                place, inside = start // quarter, start % quarter
                begin = place // 2 * quarter + inside
                value = lax.dynamic_slice_in_dim(kept, begin, unit, 0)
                if not aligned:
                    value = jnp.where(
                        place % 2 == x, value, lax.dynamic_slice_in_dim(other, begin, unit, 0)
                    )
                parts.append(value)
            columns.append(parts[0] if len(parts) == 1 else jnp.concatenate(parts, axis=0))
        rows = columns[0] if len(columns) == 1 else jnp.concatenate(columns, axis=1)
        return jnp.where(source == r, rows, jnp.zeros_like(rows))

    steps, free = [(FAR, 0, "far"), (SLAB, 0, "slab")], {}

    def send_over(link, ready, size):
        begin = max(ready, free.get(link, 0.0))
        free[link] = begin + size * UNIT
        return begin, free[link] + HOP

    clock, finals, arrivals = [], [], []
    for k, size in enumerate(sizes):
        begin, now = send_over("x", 0.0, size)
        steps.append((begin - LEAD if k else -100.0, k, "send"))
        clock.append(now)
    chain = [("in", t) for t in range(hops)] + ["middle"] + [("out", t) for t in range(hops)]
    for k, size in enumerate(sizes):
        steps.append((clock[k], k, "sum"))
        now = clock[k]
        for name in chain:
            _, now = send_over(name, now + STEP, size)
            steps.append((now, k, name))
        finals.append(now)
    for k, size in enumerate(sizes):
        _, now = send_over("x", finals[k] + STEP, size)
        arrivals.append(now)
        steps.append((now, k, "other"))
    batches = BATCHES
    for i, groups in enumerate(batches):
        needed = [k for k, runs in enumerate(pieces) if any(run[0] in groups for run in runs)]
        now = max((finals if aligned else arrivals)[k] for k in needed) + 0.01
        for t in range(len(spread) + 1):
            steps.append((now, i, ("trail", t)))
            now += HOP + STEP + UNIT * len(groups) / (t + 1)
        steps.append((now, i, "factor"))
    steps.sort(key=lambda step: step[0])
    if share % LANES == 0 and row_count == 4:
        ids = jnp.stack([jnp.stack(share_order(r)), jnp.stack(share_order(source))])
        ids, ordered = ids.astype(jnp.int32), inverse
    else:
        ids = None
        ordered = take(take(inverse, share_order(r), 0), share_order(source), 1)
    factors = []

    state, mine, others = [None] * count, [None] * count, [None] * count
    trailing = [None] * len(batches)
    def quarters(positions):
        for position in positions:
            if position not in scaled:
                scaled[position] = scaled_quarter(order, position, border, after(weights))
                done(scaled[position])
        return [scaled[position] for position in positions]

    for _, k, name in steps:
        if name in ("send", "sum"):
            used = sorted({run[1] for run in pieces[k]})
            both = quarters([2 * half + (name == "send") for half in used])
            both = [both[used.index(half)] if half in used else both[0] for half in (0, 1)]
        if name == "send" and k == 0:
            state[k] = over_scen(first_send, swap_x)
        elif name == "send":
            values = list(heads)
            for g in sorted({run[0] for run in pieces[k]}):
                values[g] = after(heads[g])
            (send,) = panel_piece(pieces[k], both, values, [], [bf16])
            done(send)
            state[k] = over_scen(send, swap_x)
        elif name == "far":
            far = list(after(*far)) if len(far) > 1 else [after(far[0])]
            done(*far)
            heads[2:] = joined(far), joined([over_row(value, 1) for value in far])
        elif name == "sum":
            out = panel_piece(pieces[k], both, heads, [after(state[k])], [f32, bf16])
            done(*out)
            state[k] = out[0], over_scen(out[1], (inward + [middle])[0])
        elif name == "middle" or name[0] == "in":
            total, got = after(*state[k])
            total = total + got.astype(f32)
            if name == "middle":
                total = total.astype(bf16)
                done(total)
                if hops:
                    state[k] = total, over_scen(total, outward[0])
                else:
                    mine[k], others[k] = total, over_scen(total, swap_x)
            else:
                done(total)
                state[k] = total, over_scen(total, (inward[1:] + [middle])[name[1]])
        elif name[0] == "out":
            t = name[1]
            final, got = after(*state[k])
            final = jnp.where(spread_to[t], got, final)
            done(final)
            if t < hops - 1:
                state[k] = final, over_scen(final, outward[t + 1])
            else:
                mine[k], others[k] = final, over_scen(final, swap_x)
        elif name == "other":
            others[k] = after(others[k])
            done(others[k])
        elif name == "slab":
            held = held_slab(order, after(slab))
            done(held)
        elif name == "factor":
            rows = after(trailing[k])
            last_one = k == len(batches) - 1
            factors = [
                factor(ids, ordered, tuple(widths), [batches[k]], [rows], factors, bf16 if last_one else f32)
            ]
            done(*factors)
        else:
            t = name[1]
            if t == 0:
                rows = trailing_rows(batches[k])
            else:
                rows, got = after(*trailing[k])
                rows = rows + got
            done(rows)
            trailing[k] = rows
            if t < len(spread):
                trailing[k] = rows, lax.ppermute(rows, ("scen", "row"), spread[t])

    places = []
    for k in range(count):
        for g, h, begin, end, at_row in offsets[k]:
            places.append((g, 0, h, begin, end, k, at_row))
            places.append((g, 1, h, begin, end, count + k, at_row))
    return update(order, held, factors[0], (tuple(widths), places), mine + others)


def solution(mesh):
    return jax.shard_map(
        body,
        mesh=mesh,
        in_specs=(P("scen", "row", None), P("scen", None), P(), P(), P(), P("row", "scen")),
        out_specs=P("row", "scen"),
        check_vma=False,
    )
```

```python
import functools

import jax
import jax.numpy as jnp
from jax import lax
from jax.experimental import pallas as pl
from jax.experimental.pallas import tpu as pltpu
from jax.sharding import PartitionSpec as P

f32, bf16 = jnp.float32, jnp.bfloat16
LANES = 128
MIB = 1 << 20
LIMIT, LIMIT_FIRST, LIMIT_REST = 10 * MIB, 54 * MIB, 50 * MIB
SEND_US, SUM_US, JOIN_US, REST_US, TAIL_US = 2.00, 2.00, 1.00, 26.64, 0.92
IN_VMEM = pl.BlockSpec(memory_space=pltpu.VMEM)
IN_HBM = pl.BlockSpec(memory_space=pltpu.HBM)
PIECES = ((2, 3, 3), (4, 4))
UNIT, HOP, STEP, FAR, SLAB, AHEAD = 2.85, 2.00, 1.50, 17.72, 88.61, 99.00
SHIFT = {'send': -1.5, 'sum': 0.0, 'far': 0.0, 'back': 0.0, 'join': 0.0, 'other': 0.0, 'trail': 0.0}
BATCHES = ((0, 1, 2), (3,))


def cost(us):
    return pl.CostEstimate(flops=int(us * 1e9), bytes_accessed=int(us * 2e6), transcendentals=0)


def nt_dot(a, b):
    return lax.dot_general(a, b, (((1,), (1,)), ((), ())), preferred_element_type=f32)


def scaled_flat(blocks, weights):
    parts = [
        (blocks[k].astype(f32) * weights[k : k + 1, :]).astype(bf16) for k in range(blocks.shape[0])
    ]
    return jnp.concatenate(parts, axis=1)


def first_kernel(
    parts, place_ref, counts_ref, order_ref, index_ref, table_ref, border_ref, *rest
):
    weights_ref, heads_ref, scaled_ref, send_ref, held_heads, held, sems = rest
    slots, quarter, width = held.shape
    share = heads_ref.shape[0]
    step = slots // parts
    first = pl.multiple_of(order_ref[1] * quarter, quarter)
    near = pltpu.make_async_copy(border_ref.at[:, pl.ds(0, share), :], held_heads, sems.at[parts])
    near.start()
    copies = [
        pltpu.make_async_copy(
            border_ref.at[pl.ds(i * step, step), pl.ds(first, quarter), :],
            held.at[pl.ds(i * step, step)],
            sems.at[i],
        )
        for i in range(parts)
    ]
    for copy in copies:
        copy.start()

    index = index_ref[...]
    high, low = index // LANES, index % LANES
    total = jnp.zeros(index.shape, f32)
    for row in range(table_ref.shape[0]):
        entries = jnp.broadcast_to(table_ref[row : row + 1, :], index.shape)
        picked = jnp.take_along_axis(entries, low, axis=1, mode="promise_in_bounds")
        total = jnp.where(high == row, picked, total)
    live = lax.broadcasted_iota(jnp.int32, index.shape, 0) < counts_ref[place_ref[0]]
    weights_ref[...] = jnp.where(live, total, 0.0)

    near.wait()
    heads_ref[...] = scaled_flat(held_heads, weights_ref[...])
    for i, copy in enumerate(copies):
        copy.wait()
        scaled_ref[:, i * step * width : (i + 1) * step * width] = scaled_flat(
            held.at[pl.ds(i * step, step)], weights_ref[i * step : (i + 1) * step, :]
        )
    send_ref[...] = nt_dot(scaled_ref[...], heads_ref[...]).astype(bf16)


def first_step(place, counts, order, col_index, barrier, border, share):
    slots, rows, width = border.shape
    quarter = rows // 4
    parts = 4 if slots % 4 == 0 else 1
    smem = pl.BlockSpec(memory_space=pltpu.SMEM)
    whole = lambda shape: pl.BlockSpec(shape, lambda i: (0,) * len(shape))
    table = barrier.reshape(-1, LANES)
    shapes = [
        jax.ShapeDtypeStruct(col_index.shape, f32),
        jax.ShapeDtypeStruct((share, slots * width), bf16),
        jax.ShapeDtypeStruct((quarter, slots * width), bf16),
        jax.ShapeDtypeStruct((quarter, share), bf16),
    ]
    return pl.pallas_call(
        functools.partial(first_kernel, parts),
        grid=(1,),
        in_specs=[smem, smem, smem, whole(col_index.shape), whole(table.shape), IN_HBM],
        out_specs=[whole(out.shape) for out in shapes],
        out_shape=shapes,
        scratch_shapes=[
            pltpu.VMEM((slots, share, width), bf16),
            pltpu.VMEM((slots, quarter, width), bf16),
            pltpu.SemaphoreType.DMA((parts + 1,)),
        ],
        cost_estimate=cost(REST_US),
        compiler_params=pltpu.CompilerParams(vmem_limit_bytes=LIMIT_FIRST),
        name="first_step",
    )(place, counts, order, col_index, table, border)


def scale_kernel(positions, parts, order_ref, border_ref, weights_ref, *rest):
    outs, held, sems = rest[: len(positions)], rest[-2], rest[-1]
    slots, rows, width = held.shape[1:]
    step = slots // parts
    copies = []
    for n, position in enumerate(positions):
        first = pl.multiple_of(order_ref[position] * rows, rows)
        copies += [
            pltpu.make_async_copy(
                border_ref.at[pl.ds(i * step, step), pl.ds(first, rows), :],
                held.at[n, pl.ds(i * step, step)],
                sems.at[n * parts + i],
            )
            for i in range(parts)
        ]
    for copy in copies:
        copy.start()
    for n, out in enumerate(outs):
        for i in range(parts):
            copies[n * parts + i].wait()
            out[:, i * step * width : (i + 1) * step * width] = scaled_flat(
                held.at[n, pl.ds(i * step, step)], weights_ref[i * step : (i + 1) * step, :]
            )


def scaled_quarters(order, positions, border, weights):
    slots, rows, width = border.shape
    quarter = rows // 4
    parts = 4 if slots % 4 == 0 else 1
    count = len(positions)
    return pl.pallas_call(
        functools.partial(scale_kernel, positions, parts),
        in_specs=[pl.BlockSpec(memory_space=pltpu.SMEM), IN_HBM, IN_VMEM],
        out_specs=[IN_VMEM] * count,
        out_shape=[jax.ShapeDtypeStruct((quarter, slots * width), bf16)] * count,
        scratch_shapes=[
            pltpu.VMEM((count, slots, quarter, width), bf16),
            pltpu.SemaphoreType.DMA((count * parts,)),
        ],
        cost_estimate=cost(REST_US),
        compiler_params=pltpu.CompilerParams(vmem_limit_bytes=LIMIT_REST),
        name="scaled_quarters",
    )(order, border, weights)


def piece_rows(runs, rows_refs, heads_refs, got, store):
    groups = sorted({g for g, _, _, _ in runs})
    at = 0
    for g, half, begin, end in runs:
        value = nt_dot(rows_refs[half][begin:end, :], heads_refs[groups.index(g)][...])
        place = slice(at, at + end - begin)
        if got is not None:
            value += got[place, :].astype(f32)
        store[place, :] = value.astype(store.dtype)
        at += end - begin


def send_kernel(runs, *refs):
    piece_rows(runs, refs[:2], refs[2:-1], None, refs[-1])


def sum_kernel(runs, part_ref, *refs):
    *heads, got, keep_ref, send_ref, total = refs[2:]
    piece_rows(runs, refs[:2], heads, got, total)
    half = keep_ref.shape[0]
    part = part_ref[0]
    keep_ref[...] = total[pl.ds(pl.multiple_of(part * half, half), half), :]
    send_ref[...] = total[pl.ds(pl.multiple_of((1 - part) * half, half), half), :].astype(bf16)


def piece_shape(runs, heads):
    groups = sorted({g for g, _, _, _ in runs})
    rows = sum(end - begin for _, _, begin, end in runs)
    return [heads[g] for g in groups], rows, heads[groups[0]].shape[0]


def piece_to_send(runs, scaled, heads):
    used, rows, columns = piece_shape(runs, heads)
    return pl.pallas_call(
        functools.partial(send_kernel, runs),
        in_specs=[IN_VMEM] * (2 + len(used)),
        out_specs=IN_VMEM,
        out_shape=jax.ShapeDtypeStruct((rows, columns), bf16),
        cost_estimate=cost(SEND_US),
        compiler_params=pltpu.CompilerParams(vmem_limit_bytes=LIMIT),
        name="piece_to_send",
    )(*scaled, *used)


def piece_sum(runs, part, scaled, heads, got):
    used, rows, columns = piece_shape(runs, heads)
    return pl.pallas_call(
        functools.partial(sum_kernel, runs),
        in_specs=[pl.BlockSpec(memory_space=pltpu.SMEM)] + [IN_VMEM] * (3 + len(used)),
        out_specs=[IN_VMEM] * 2,
        out_shape=[jax.ShapeDtypeStruct((rows // 2, columns), kind) for kind in (f32, bf16)],
        scratch_shapes=[pltpu.VMEM((rows, columns), f32)],
        cost_estimate=cost(SUM_US),
        compiler_params=pltpu.CompilerParams(vmem_limit_bytes=LIMIT),
        name="piece_sum",
    )(part, *scaled, *used, got)


def join_kernel(part_ref, own_ref, got_ref, out_ref):
    half = own_ref.shape[0]
    part = part_ref[0]
    out_ref[pl.ds(pl.multiple_of(part * half, half), half), :] = own_ref[...]
    out_ref[pl.ds(pl.multiple_of((1 - part) * half, half), half), :] = got_ref[...]


def join_halves(part, own, got):
    rows, columns = own.shape
    return pl.pallas_call(
        join_kernel,
        in_specs=[pl.BlockSpec(memory_space=pltpu.SMEM), IN_VMEM, IN_VMEM],
        out_specs=IN_VMEM,
        out_shape=jax.ShapeDtypeStruct((2 * rows, columns), own.dtype),
        cost_estimate=cost(JOIN_US),
        compiler_params=pltpu.CompilerParams(vmem_limit_bytes=LIMIT),
        name="join_halves",
    )(part, own, got)


def hold_kernel(order_ref, slab_ref, out_ref, sems):
    quarter = out_ref.shape[1]
    copies = []
    for p in range(4):
        rows = pl.ds(pl.multiple_of(order_ref[p] * quarter, quarter), quarter)
        copies.append(pltpu.make_async_copy(slab_ref.at[rows], out_ref.at[p], sems.at[p]))
    for copy in copies:
        copy.start()
    for copy in copies:
        copy.wait()


def held_slab(order, slab):
    rows, columns = slab.shape
    return pl.pallas_call(
        hold_kernel,
        in_specs=[pl.BlockSpec(memory_space=pltpu.SMEM), IN_HBM],
        out_specs=IN_VMEM,
        out_shape=jax.ShapeDtypeStruct((4, rows // 4, columns), slab.dtype),
        scratch_shapes=[pltpu.SemaphoreType.DMA((4,))],
        cost_estimate=cost(REST_US),
        compiler_params=pltpu.CompilerParams(vmem_limit_bytes=LIMIT),
        name="held_slab",
    )(order, slab)


def factor_kernel(plan, ids_ref, inverse_ref, *rest):
    widths, sources = plan
    n = len(widths)
    trailing, rest = rest[: len(sources)], rest[len(sources) :]
    total_ref, out_ref = rest if len(rest) == 2 else (None, rest[0])
    ends = [sum(widths[:g]) for g in range(n + 1)]
    begin_of = lambda which, g: (
        ends[g] if ids_ref is None else pl.multiple_of(ids_ref[which, g] * widths[g], widths[g])
    )
    for g in range(n):
        total = None if total_ref is None else total_ref[ends[g] : ends[g + 1], :]
        for batch, groups in enumerate(sources):
            begin = 0
            for j in groups:
                block = inverse_ref[pl.ds(begin_of(0, g), widths[g]), pl.ds(begin_of(1, j), widths[j])]
                part = nt_dot(block, trailing[batch][:, begin : begin + widths[j]])
                total = part if total is None else total + part
                begin += widths[j]
        out_ref[ends[g] : ends[g + 1], :] = total.astype(out_ref.dtype)


def factor(ids, inverse, widths, sources, trailing, total, kind):
    smem = pl.BlockSpec(memory_space=pltpu.SMEM)

    def kernel(*refs):
        factor_kernel((widths, sources), *((None, *refs) if ids is None else refs))

    operands = ([] if ids is None else [ids]) + [inverse, *trailing, *total]
    return pl.pallas_call(
        kernel,
        in_specs=([] if ids is None else [smem]) + [IN_VMEM] * (1 + len(trailing) + len(total)),
        out_specs=IN_VMEM,
        out_shape=jax.ShapeDtypeStruct((inverse.shape[0], trailing[0].shape[0]), kind),
        cost_estimate=cost(TAIL_US),
        compiler_params=pltpu.CompilerParams(vmem_limit_bytes=LIMIT),
        name="factor",
    )(*operands)


def update_kernel(plan, order_ref, slab_ref, factor_ref, *rest):
    widths, places = plan
    *pieces, out_ref, held, sems = rest
    quarter = held.shape[1]
    ends = [sum(widths[:g]) for g in range(len(widths) + 1)]
    stores = []
    for p in range(4):
        rows = pl.ds(pl.multiple_of(order_ref[p] * quarter, quarter), quarter)
        stores.append(pltpu.make_async_copy(held.at[p], out_ref.at[rows], sems.at[p]))
    for p in range(4):
        held[p] = slab_ref[p]
        for g, side, half, begin, end, piece, at in places:
            if 2 * half + side == p:
                held[p, begin:end, :] -= jnp.dot(
                    pieces[piece][at : at + end - begin, :],
                    factor_ref[ends[g] : ends[g + 1], :],
                    preferred_element_type=f32,
                )
        stores[p].start()
    for store in stores:
        store.wait()


def update(order, held, factor_value, plan, pieces):
    _, quarter, columns = held.shape
    return pl.pallas_call(
        functools.partial(update_kernel, plan),
        in_specs=[pl.BlockSpec(memory_space=pltpu.SMEM)] + [IN_VMEM] * (2 + len(pieces)),
        out_specs=IN_HBM,
        out_shape=jax.ShapeDtypeStruct((4 * quarter, columns), held.dtype),
        scratch_shapes=[
            pltpu.VMEM(held.shape, f32),
            pltpu.SemaphoreType.DMA((4,)),
        ],
        cost_estimate=cost(TAIL_US),
        compiler_params=pltpu.CompilerParams(vmem_limit_bytes=LIMIT),
        name="update",
    )(order, held, factor_value, *pieces)


def body(border, col_index, barrier, counts, inverse, slab):
    scen_count, row_count = lax.axis_size("scen"), lax.axis_size("row")
    s, r = lax.axis_index("scen"), lax.axis_index("row")
    slots, local_rows, width = border.shape
    panel_width = inverse.shape[0]
    share = panel_width // row_count
    quarter = local_rows // 4
    trail = slab.shape[1]
    x, z = s % 2, s // 2
    order = jnp.stack([x, 1 - x, 2 + x, 3 - x]).astype(jnp.int32)

    masks = [1 << bit for bit in range((scen_count - 1).bit_length())]
    part = (z % 2).astype(jnp.int32).reshape(1)
    over_scen = lambda value, mask: lax.ppermute(
        value.astype(bf16), "scen", [(i, i ^ mask) for i in range(scen_count)]
    )
    over_row = lambda value, mask: lax.ppermute(
        value, "row", [(i, i ^ mask) for i in range(row_count)]
    )

    last = []

    def after(*values):
        if not last:
            return values if len(values) > 1 else values[0]
        out = lax.optimization_barrier((*values, *last))
        return out[: len(values)] if len(values) > 1 else out[0]

    def done(*values):
        last[:] = values

    place = s.astype(jnp.int32).reshape(1)
    weights, own, scaled_sent, first_send = first_step(
        place, counts, order, col_index, barrier, border, share
    )
    scaled = {1: scaled_sent}
    done(own)
    far = [over_row(own, mask) for mask in range(2, row_count, 2)]
    sibling = over_row(own, 1)
    joined = lambda group: group[0] if len(group) == 1 else jnp.concatenate(group, axis=0)
    heads = [own, sibling, None, None]
    widths = [share, share, share * len(far), share * len(far)]

    def share_order(device):
        masks = [0, 1] + list(range(2, row_count, 2)) + list(range(3, row_count, 2))
        return [device ^ mask for mask in masks]

    first_row = s * trail
    source = first_row // local_rows

    def take(value, shares, axis):
        return jnp.concatenate(
            [lax.dynamic_slice_in_dim(value, k * share, share, axis) for k in shares], axis
        )

    aligned = trail <= quarter and all(
        (g * trail) % local_rows // quarter % 2 == g % 2 for g in range(scen_count)
    )
    unit = min(trail, quarter)
    row_masks = [1 << k for k in reversed(range((row_count - 1).bit_length()))]
    spread = []
    reached = {g: {g * trail // local_rows} for g in range(scen_count)}
    for mask in row_masks:
        spread.append(
            [
                (g * row_count + k, g * row_count + (k ^ mask))
                for g in range(scen_count)
                for k in sorted(reached[g])
            ]
        )
        for g in range(scen_count):
            reached[g] |= {k ^ mask for k in reached[g]}

    eighth = quarter // 2
    pieces = []
    for pair, sizes in enumerate(PIECES):
        units = [(2 * pair + g, b // 2, b % 2) for g in range(2) for b in range(4)]
        for size in sizes:
            runs = []
            for g, half, spot in units[:size]:
                if runs and runs[-1][:2] == (g, half):
                    runs[-1] = (*runs[-1][:3], (spot + 1) * eighth)
                else:
                    runs.append((g, half, spot * eighth, (spot + 1) * eighth))
            pieces.append(runs)
            units = units[size:]
    sizes = [size for pair in PIECES for size in pair]
    count = len(pieces)
    offsets = []
    for runs in pieces:
        places, at_row = [], 0
        for g, h, begin, end in runs:
            places.append((g, h, begin, end, at_row))
            at_row += end - begin
        offsets.append(places)
    last_of = [max(k for k, runs in enumerate(pieces) if any(run[0] == g for run in runs)) for g in range(4)]

    def kept_rows(values, g):
        parts = []
        for k, places in enumerate(offsets):
            parts += [values[k][at : at + end - begin] for h, _, begin, end, at in places if h == g]
        return jnp.concatenate(parts, axis=0)

    def trailing_rows(groups):
        columns = []
        for g in groups:
            kept, parts = kept_rows(mine, g), []
            other = None if aligned else kept_rows(others, g)
            for i in range(trail // unit):
                start = first_row % local_rows + i * unit
                place, inside = start // quarter, start % quarter
                begin = place // 2 * quarter + inside
                value = lax.dynamic_slice_in_dim(kept, begin, unit, 0)
                if not aligned:
                    value = jnp.where(
                        place % 2 == x, value, lax.dynamic_slice_in_dim(other, begin, unit, 0)
                    )
                parts.append(value)
            columns.append(parts[0] if len(parts) == 1 else jnp.concatenate(parts, axis=0))
        rows = columns[0] if len(columns) == 1 else jnp.concatenate(columns, axis=1)
        return jnp.where(source == r, rows, jnp.zeros_like(rows))

    steps, free = [(FAR, 0, "heads"), (SLAB, 0, "slab")], {}

    def send_over(link, ready, size):
        begin = max(ready, free.get(link, 0.0))
        free[link] = begin + size * UNIT
        return begin, free[link] + HOP

    clock, finals, arrivals = [], [], []
    for k, size in enumerate(sizes):
        begin, now = send_over("x", 0.0, size)
        late = any(run[0] >= 2 for run in pieces[k])
        when = max(begin + SHIFT["send"], FAR + 0.01) if late else begin + SHIFT["send"]
        steps.append((when if k else -100.0, k, "send"))
        clock.append(now)
    hops = len(masks)
    for k, size in enumerate(sizes):
        steps.append((clock[k] + SHIFT["sum"], k, "sum"))
        _, now = send_over("pair", clock[k] + STEP, size / 2)
        for t in range(2, hops):
            steps.append((now + SHIFT["far"], k, ("far", t)))
            _, now = send_over(("far", t), now + STEP, size)
        steps.append((now + SHIFT["back"], k, "back"))
        _, now = send_over("pair back", now + STEP, size / 2)
        steps.append((now + SHIFT["join"], k, "join"))
        finals.append(now)
    for k, size in enumerate(sizes):
        _, now = send_over("x", finals[k] + STEP, size)
        arrivals.append(now)
    batches, ends = BATCHES, []
    for i, groups in enumerate(batches):
        needed = [k for k, runs in enumerate(pieces) if any(run[0] in groups for run in runs)]
        now = max((finals if aligned else arrivals)[k] for k in needed) + 0.01 + SHIFT["trail"]
        for t in range(len(spread) + 1):
            steps.append((now, i, ("trail", t)))
            ends.append(now)
            now += HOP + STEP + UNIT * len(groups) / (t + 1)
        steps.append((ends[-1] + 0.01, i, "factor"))
    for k, now in enumerate(arrivals):
        now = now + SHIFT["other"] if k < count - 1 or not aligned else min(now, ends[-1] + AHEAD)
        steps.append((now, k, "other"))
    steps.sort(key=lambda step: step[0])
    if share % LANES == 0 and row_count == 4:
        ids = jnp.stack([jnp.stack(share_order(r)), jnp.stack(share_order(source))])
        ids, ordered = ids.astype(jnp.int32), inverse
    else:
        ids = None
        ordered = take(take(inverse, share_order(r), 0), share_order(source), 1)
    factors = []

    state, mine, others = [None] * count, [None] * count, [None] * count
    trailing = [None] * len(batches)
    rest = (3, 0, 2)
    scaled.update(zip(rest, scaled_quarters(order, rest, border, after(weights))))
    done(*(scaled[position] for position in rest))

    for _, k, name in steps:
        if name in ("send", "sum"):
            both = [scaled[2 * half + (name == "send")] for half in (0, 1)]
        if name == "send" and k == 0:
            state[k] = over_scen(first_send, 1)
        elif name == "send":
            values = list(heads)
            for g in sorted({run[0] for run in pieces[k]}):
                values[g] = after(heads[g])
            send = piece_to_send(pieces[k], both, values)
            done(send)
            state[k] = over_scen(send, 1)
        elif name == "heads":
            far = list(after(*far)) if len(far) > 1 else [after(far[0])]
            done(*far)
            heads[2:] = joined(far), joined([over_row(value, 1) for value in far])
        elif name == "sum":
            keep, send = piece_sum(pieces[k], part, both, heads, after(state[k]))
            done(keep, send)
            state[k] = keep, over_scen(send, 2)
        elif name[0] == "far" or name == "back":
            total, got = after(*state[k])
            total = total + got.astype(f32)
            if name == "back":
                total = total.astype(bf16)
            done(total)
            state[k] = total, over_scen(total, 2 if name == "back" else masks[name[1]])
        elif name == "join":
            mine[k] = join_halves(part, *after(*state[k]))
            done(mine[k])
            others[k] = over_scen(mine[k], 1)
        elif name == "other":
            others[k] = after(others[k])
            done(others[k])
        elif name == "slab":
            held = held_slab(order, after(slab))
            done(held)
        elif name == "factor":
            rows = after(trailing[k])
            last_one = k == len(batches) - 1
            factors = [
                factor(ids, ordered, tuple(widths), [batches[k]], [rows], factors, bf16 if last_one else f32)
            ]
            done(*factors)
        else:
            t = name[1]
            if t == 0:
                rows = trailing_rows(batches[k])
            else:
                rows, got = after(*trailing[k])
                rows = rows + got
            done(rows)
            trailing[k] = rows
            if t < len(spread):
                trailing[k] = rows, lax.ppermute(rows, ("scen", "row"), spread[t])

    places = []
    for k in range(count):
        for g, h, begin, end, at_row in offsets[k]:
            places.append((g, 0, h, begin, end, k, at_row))
            places.append((g, 1, h, begin, end, count + k, at_row))
    return update(order, held, factors[0], (tuple(widths), places), mine + others)


def solution(mesh):
    return jax.shard_map(
        body,
        mesh=mesh,
        in_specs=(P("scen", "row", None), P("scen", None), P(), P(), P(), P("row", "scen")),
        out_specs=P("row", "scen"),
        check_vma=False,
    )
```

```python
import functools

import jax
import jax.numpy as jnp
from jax import lax
from jax.experimental import pallas as pl
from jax.experimental.pallas import tpu as pltpu
from jax.sharding import PartitionSpec as P

f32, bf16 = jnp.float32, jnp.bfloat16
LANES = 128
MIB = 1 << 20
LIMIT, LIMIT_FIRST, LIMIT_REST = 10 * MIB, 54 * MIB, 50 * MIB
SEND_US, SUM_US, JOIN_US, REST_US, TAIL_US = 2.00, 0.54, 1.00, 26.64, 0.92
IN_VMEM = pl.BlockSpec(memory_space=pltpu.VMEM)
IN_HBM = pl.BlockSpec(memory_space=pltpu.HBM)
PIECES = ((2, 3, 3), (4, 4))
UNIT, HOP, STEP, FAR, SLAB, AHEAD = 2.85, 2.00, 1.50, 17.72, 83.09, 99.00
KEPT = 6.00
SHIFT = {'send': -1.5, 'sum': 1.32, 'far': 0.0, 'back': 0.0, 'join': 0.0, 'other': 0.0, 'trail': 0.0}
BATCHES = ((0, 1, 2), (3,))


def cost(us):
    return pl.CostEstimate(flops=int(us * 1e9), bytes_accessed=int(us * 2e6), transcendentals=0)


def nt_dot(a, b):
    return lax.dot_general(a, b, (((1,), (1,)), ((), ())), preferred_element_type=f32)


def scaled_flat(blocks, weights):
    parts = [
        (blocks[k].astype(f32) * weights[k : k + 1, :]).astype(bf16) for k in range(blocks.shape[0])
    ]
    return jnp.concatenate(parts, axis=1)


def first_kernel(
    parts, place_ref, counts_ref, order_ref, index_ref, table_ref, border_ref, *rest
):
    weights_ref, heads_ref, scaled_ref, send_ref, held_heads, held, sems = rest
    slots, quarter, width = held.shape
    share = heads_ref.shape[0]
    step = slots // parts
    first = pl.multiple_of(order_ref[1] * quarter, quarter)
    near = pltpu.make_async_copy(border_ref.at[:, pl.ds(0, share), :], held_heads, sems.at[parts])
    near.start()
    copies = [
        pltpu.make_async_copy(
            border_ref.at[pl.ds(i * step, step), pl.ds(first, quarter), :],
            held.at[pl.ds(i * step, step)],
            sems.at[i],
        )
        for i in range(parts)
    ]
    for copy in copies:
        copy.start()

    index = index_ref[...]
    high, low = index // LANES, index % LANES
    total = jnp.zeros(index.shape, f32)
    for row in range(table_ref.shape[0]):
        entries = jnp.broadcast_to(table_ref[row : row + 1, :], index.shape)
        picked = jnp.take_along_axis(entries, low, axis=1, mode="promise_in_bounds")
        total = jnp.where(high == row, picked, total)
    live = lax.broadcasted_iota(jnp.int32, index.shape, 0) < counts_ref[place_ref[0]]
    weights_ref[...] = jnp.where(live, total, 0.0)

    near.wait()
    heads_ref[...] = scaled_flat(held_heads, weights_ref[...])
    for i, copy in enumerate(copies):
        copy.wait()
        scaled_ref[:, i * step * width : (i + 1) * step * width] = scaled_flat(
            held.at[pl.ds(i * step, step)], weights_ref[i * step : (i + 1) * step, :]
        )
    send_ref[...] = nt_dot(scaled_ref[...], heads_ref[...]).astype(bf16)


def first_step(place, counts, order, col_index, barrier, border, share):
    slots, rows, width = border.shape
    quarter = rows // 4
    parts = 4 if slots % 4 == 0 else 1
    smem = pl.BlockSpec(memory_space=pltpu.SMEM)
    whole = lambda shape: pl.BlockSpec(shape, lambda i: (0,) * len(shape))
    table = barrier.reshape(-1, LANES)
    shapes = [
        jax.ShapeDtypeStruct(col_index.shape, f32),
        jax.ShapeDtypeStruct((share, slots * width), bf16),
        jax.ShapeDtypeStruct((quarter, slots * width), bf16),
        jax.ShapeDtypeStruct((quarter, share), bf16),
    ]
    return pl.pallas_call(
        functools.partial(first_kernel, parts),
        grid=(1,),
        in_specs=[smem, smem, smem, whole(col_index.shape), whole(table.shape), IN_HBM],
        out_specs=[whole(out.shape) for out in shapes],
        out_shape=shapes,
        scratch_shapes=[
            pltpu.VMEM((slots, share, width), bf16),
            pltpu.VMEM((slots, quarter, width), bf16),
            pltpu.SemaphoreType.DMA((parts + 1,)),
        ],
        cost_estimate=cost(REST_US),
        compiler_params=pltpu.CompilerParams(vmem_limit_bytes=LIMIT_FIRST),
        name="first_step",
    )(place, counts, order, col_index, table, border)


def scale_kernel(positions, parts, order_ref, border_ref, weights_ref, *rest):
    outs, held, sems = rest[: len(positions)], rest[-2], rest[-1]
    slots, rows, width = held.shape[1:]
    step = slots // parts
    copies = []
    for n, position in enumerate(positions):
        first = pl.multiple_of(order_ref[position] * rows, rows)
        copies += [
            pltpu.make_async_copy(
                border_ref.at[pl.ds(i * step, step), pl.ds(first, rows), :],
                held.at[n, pl.ds(i * step, step)],
                sems.at[n * parts + i],
            )
            for i in range(parts)
        ]
    for copy in copies:
        copy.start()
    for n, out in enumerate(outs):
        for i in range(parts):
            copies[n * parts + i].wait()
            out[:, i * step * width : (i + 1) * step * width] = scaled_flat(
                held.at[n, pl.ds(i * step, step)], weights_ref[i * step : (i + 1) * step, :]
            )


def scaled_quarters(order, positions, border, weights):
    slots, rows, width = border.shape
    quarter = rows // 4
    parts = 4 if slots % 4 == 0 else 1
    count = len(positions)
    return pl.pallas_call(
        functools.partial(scale_kernel, positions, parts),
        in_specs=[pl.BlockSpec(memory_space=pltpu.SMEM), IN_HBM, IN_VMEM],
        out_specs=[IN_VMEM] * count,
        out_shape=[jax.ShapeDtypeStruct((quarter, slots * width), bf16)] * count,
        scratch_shapes=[
            pltpu.VMEM((count, slots, quarter, width), bf16),
            pltpu.SemaphoreType.DMA((count * parts,)),
        ],
        cost_estimate=cost(REST_US),
        compiler_params=pltpu.CompilerParams(vmem_limit_bytes=LIMIT_REST),
        name="scaled_quarters",
    )(order, border, weights)


def piece_rows(runs, rows_refs, heads_refs, got, store):
    groups = sorted({g for g, _, _, _ in runs})
    at = 0
    for g, half, begin, end in runs:
        value = nt_dot(rows_refs[half][begin:end, :], heads_refs[groups.index(g)][...])
        place = slice(at, at + end - begin)
        if got is not None:
            value += got[place, :].astype(f32)
        store[place, :] = value.astype(store.dtype)
        at += end - begin


def send_kernel(runs, *refs):
    piece_rows(runs, refs[:2], refs[2:-1], None, refs[-1])


def sum_kernel(runs, part_ref, *refs):
    *heads, got, keep_ref, send_ref, total = refs[2:]
    piece_rows(runs, refs[:2], heads, got, total)
    half = keep_ref.shape[0]
    part = part_ref[0]
    keep_ref[...] = total[pl.ds(pl.multiple_of(part * half, half), half), :]
    send_ref[...] = total[pl.ds(pl.multiple_of((1 - part) * half, half), half), :].astype(bf16)


def piece_shape(runs, heads):
    groups = sorted({g for g, _, _, _ in runs})
    rows = sum(end - begin for _, _, begin, end in runs)
    return [heads[g] for g in groups], rows, heads[groups[0]].shape[0]


def piece_to_send(runs, scaled, heads):
    used, rows, columns = piece_shape(runs, heads)
    return pl.pallas_call(
        functools.partial(send_kernel, runs),
        in_specs=[IN_VMEM] * (2 + len(used)),
        out_specs=IN_VMEM,
        out_shape=jax.ShapeDtypeStruct((rows, columns), bf16),
        cost_estimate=cost(SEND_US),
        compiler_params=pltpu.CompilerParams(vmem_limit_bytes=LIMIT),
        name="piece_to_send",
    )(*scaled, *used)


def piece_sum(runs, part, scaled, heads, got):
    used, rows, columns = piece_shape(runs, heads)
    return pl.pallas_call(
        functools.partial(sum_kernel, runs),
        in_specs=[pl.BlockSpec(memory_space=pltpu.SMEM)] + [IN_VMEM] * (3 + len(used)),
        out_specs=[IN_VMEM] * 2,
        out_shape=[jax.ShapeDtypeStruct((rows // 2, columns), kind) for kind in (f32, bf16)],
        scratch_shapes=[pltpu.VMEM((rows, columns), f32)],
        cost_estimate=cost(SUM_US),
        compiler_params=pltpu.CompilerParams(vmem_limit_bytes=LIMIT),
        name="piece_sum",
    )(part, *scaled, *used, got)


def join_kernel(part_ref, own_ref, got_ref, out_ref):
    half = own_ref.shape[0]
    part = part_ref[0]
    out_ref[pl.ds(pl.multiple_of(part * half, half), half), :] = own_ref[...]
    out_ref[pl.ds(pl.multiple_of((1 - part) * half, half), half), :] = got_ref[...]


def join_halves(part, own, got):
    rows, columns = own.shape
    return pl.pallas_call(
        join_kernel,
        in_specs=[pl.BlockSpec(memory_space=pltpu.SMEM), IN_VMEM, IN_VMEM],
        out_specs=IN_VMEM,
        out_shape=jax.ShapeDtypeStruct((2 * rows, columns), own.dtype),
        cost_estimate=cost(JOIN_US),
        compiler_params=pltpu.CompilerParams(vmem_limit_bytes=LIMIT),
        name="join_halves",
    )(part, own, got)


def hold_kernel(order_ref, slab_ref, out_ref, sems):
    quarter = out_ref.shape[1]
    copies = []
    for p in range(4):
        rows = pl.ds(pl.multiple_of(order_ref[p] * quarter, quarter), quarter)
        copies.append(pltpu.make_async_copy(slab_ref.at[rows], out_ref.at[p], sems.at[p]))
    for copy in copies:
        copy.start()
    for copy in copies:
        copy.wait()


def held_slab(order, slab):
    rows, columns = slab.shape
    return pl.pallas_call(
        hold_kernel,
        in_specs=[pl.BlockSpec(memory_space=pltpu.SMEM), IN_HBM],
        out_specs=IN_VMEM,
        out_shape=jax.ShapeDtypeStruct((4, rows // 4, columns), slab.dtype),
        scratch_shapes=[pltpu.SemaphoreType.DMA((4,))],
        cost_estimate=cost(REST_US),
        compiler_params=pltpu.CompilerParams(vmem_limit_bytes=LIMIT),
        name="held_slab",
    )(order, slab)


def factor_kernel(plan, ids_ref, inverse_ref, *rest):
    widths, sources = plan
    n = len(widths)
    trailing, rest = rest[: len(sources)], rest[len(sources) :]
    total_ref, out_ref = rest if len(rest) == 2 else (None, rest[0])
    ends = [sum(widths[:g]) for g in range(n + 1)]
    begin_of = lambda which, g: (
        ends[g] if ids_ref is None else pl.multiple_of(ids_ref[which, g] * widths[g], widths[g])
    )
    for g in range(n):
        total = None if total_ref is None else total_ref[ends[g] : ends[g + 1], :]
        for batch, groups in enumerate(sources):
            begin = 0
            for j in groups:
                block = inverse_ref[pl.ds(begin_of(0, g), widths[g]), pl.ds(begin_of(1, j), widths[j])]
                part = nt_dot(block, trailing[batch][:, begin : begin + widths[j]])
                total = part if total is None else total + part
                begin += widths[j]
        out_ref[ends[g] : ends[g + 1], :] = total.astype(out_ref.dtype)


def factor(ids, inverse, widths, sources, trailing, total, kind):
    smem = pl.BlockSpec(memory_space=pltpu.SMEM)

    def kernel(*refs):
        factor_kernel((widths, sources), *((None, *refs) if ids is None else refs))

    operands = ([] if ids is None else [ids]) + [inverse, *trailing, *total]
    return pl.pallas_call(
        kernel,
        in_specs=([] if ids is None else [smem]) + [IN_VMEM] * (1 + len(trailing) + len(total)),
        out_specs=IN_VMEM,
        out_shape=jax.ShapeDtypeStruct((inverse.shape[0], trailing[0].shape[0]), kind),
        cost_estimate=cost(TAIL_US),
        compiler_params=pltpu.CompilerParams(vmem_limit_bytes=LIMIT),
        name="factor",
    )(*operands)


def update_kernel(plan, order_ref, slab_ref, factor_ref, *rest):
    widths, places = plan
    *pieces, out_ref, held, sems = rest
    quarter = held.shape[1]
    ends = [sum(widths[:g]) for g in range(len(widths) + 1)]
    stores = []
    for p in range(4):
        rows = pl.ds(pl.multiple_of(order_ref[p] * quarter, quarter), quarter)
        stores.append(pltpu.make_async_copy(held.at[p], out_ref.at[rows], sems.at[p]))
    for p in range(4):
        held[p] = slab_ref[p]
        for g, side, half, begin, end, piece, at in places:
            if 2 * half + side == p:
                held[p, begin:end, :] -= jnp.dot(
                    pieces[piece][at : at + end - begin, :],
                    factor_ref[ends[g] : ends[g + 1], :],
                    preferred_element_type=f32,
                )
        stores[p].start()
    for store in stores:
        store.wait()


def update(order, held, factor_value, plan, pieces):
    _, quarter, columns = held.shape
    return pl.pallas_call(
        functools.partial(update_kernel, plan),
        in_specs=[pl.BlockSpec(memory_space=pltpu.SMEM)] + [IN_VMEM] * (2 + len(pieces)),
        out_specs=IN_HBM,
        out_shape=jax.ShapeDtypeStruct((4 * quarter, columns), held.dtype),
        scratch_shapes=[
            pltpu.VMEM(held.shape, f32),
            pltpu.SemaphoreType.DMA((4,)),
        ],
        cost_estimate=cost(TAIL_US),
        compiler_params=pltpu.CompilerParams(vmem_limit_bytes=LIMIT),
        name="update",
    )(order, held, factor_value, *pieces)


def body(border, col_index, barrier, counts, inverse, slab):
    scen_count, row_count = lax.axis_size("scen"), lax.axis_size("row")
    s, r = lax.axis_index("scen"), lax.axis_index("row")
    slots, local_rows, width = border.shape
    panel_width = inverse.shape[0]
    share = panel_width // row_count
    quarter = local_rows // 4
    trail = slab.shape[1]
    x, z = s % 2, s // 2
    order = jnp.stack([x, 1 - x, 2 + x, 3 - x]).astype(jnp.int32)

    masks = [1 << bit for bit in range((scen_count - 1).bit_length())]
    part = (z % 2).astype(jnp.int32).reshape(1)
    over_scen = lambda value, mask: lax.ppermute(
        value.astype(bf16), "scen", [(i, i ^ mask) for i in range(scen_count)]
    )
    over_row = lambda value, mask: lax.ppermute(
        value, "row", [(i, i ^ mask) for i in range(row_count)]
    )

    last = []

    def after(*values):
        if not last:
            return values if len(values) > 1 else values[0]
        out = lax.optimization_barrier((*values, *last))
        return out[: len(values)] if len(values) > 1 else out[0]

    def done(*values):
        last[:] = values

    place = s.astype(jnp.int32).reshape(1)
    weights, own, scaled_sent, first_send = first_step(
        place, counts, order, col_index, barrier, border, share
    )
    scaled = {1: scaled_sent}
    done(own)
    far = [over_row(own, mask) for mask in range(2, row_count, 2)]
    sibling = over_row(own, 1)
    joined = lambda group: group[0] if len(group) == 1 else jnp.concatenate(group, axis=0)
    heads = [own, sibling, None, None]
    widths = [share, share, share * len(far), share * len(far)]

    def share_order(device):
        masks = [0, 1] + list(range(2, row_count, 2)) + list(range(3, row_count, 2))
        return [device ^ mask for mask in masks]

    first_row = s * trail
    source = first_row // local_rows

    def take(value, shares, axis):
        return jnp.concatenate(
            [lax.dynamic_slice_in_dim(value, k * share, share, axis) for k in shares], axis
        )

    aligned = trail <= quarter and all(
        (g * trail) % local_rows // quarter % 2 == g % 2 for g in range(scen_count)
    )
    unit = min(trail, quarter)
    row_masks = [1 << k for k in reversed(range((row_count - 1).bit_length()))]
    spread = []
    reached = {g: {g * trail // local_rows} for g in range(scen_count)}
    for mask in row_masks:
        spread.append(
            [
                (g * row_count + k, g * row_count + (k ^ mask))
                for g in range(scen_count)
                for k in sorted(reached[g])
            ]
        )
        for g in range(scen_count):
            reached[g] |= {k ^ mask for k in reached[g]}

    eighth = quarter // 2
    pieces = []
    for pair, sizes in enumerate(PIECES):
        units = [(2 * pair + g, b // 2, b % 2) for g in range(2) for b in range(4)]
        for size in sizes:
            runs = []
            for g, half, spot in units[:size]:
                if runs and runs[-1][:2] == (g, half):
                    runs[-1] = (*runs[-1][:3], (spot + 1) * eighth)
                else:
                    runs.append((g, half, spot * eighth, (spot + 1) * eighth))
            pieces.append(runs)
            units = units[size:]
    sizes = [size for pair in PIECES for size in pair]
    count = len(pieces)
    offsets = []
    for runs in pieces:
        places, at_row = [], 0
        for g, h, begin, end in runs:
            places.append((g, h, begin, end, at_row))
            at_row += end - begin
        offsets.append(places)
    last_of = [max(k for k, runs in enumerate(pieces) if any(run[0] == g for run in runs)) for g in range(4)]

    def kept_rows(values, g):
        parts = []
        for k, places in enumerate(offsets):
            parts += [values[k][at : at + end - begin] for h, _, begin, end, at in places if h == g]
        return jnp.concatenate(parts, axis=0)

    def trailing_rows(groups):
        columns = []
        for g in groups:
            kept, parts = kept_rows(mine, g), []
            other = None if aligned else kept_rows(others, g)
            for i in range(trail // unit):
                start = first_row % local_rows + i * unit
                place, inside = start // quarter, start % quarter
                begin = place // 2 * quarter + inside
                value = lax.dynamic_slice_in_dim(kept, begin, unit, 0)
                if not aligned:
                    value = jnp.where(
                        place % 2 == x, value, lax.dynamic_slice_in_dim(other, begin, unit, 0)
                    )
                parts.append(value)
            columns.append(parts[0] if len(parts) == 1 else jnp.concatenate(parts, axis=0))
        rows = columns[0] if len(columns) == 1 else jnp.concatenate(columns, axis=1)
        return jnp.where(source == r, rows, jnp.zeros_like(rows))

    steps, free = [(FAR, 0, "heads"), (SLAB, 0, "slab"), (KEPT, 0, "kept")], {}

    def send_over(link, ready, size):
        begin = max(ready, free.get(link, 0.0))
        free[link] = begin + size * UNIT
        return begin, free[link] + HOP

    clock, finals, arrivals = [], [], []
    for k, size in enumerate(sizes):
        begin, now = send_over("x", 0.0, size)
        late = any(run[0] >= 2 for run in pieces[k])
        when = max(begin + SHIFT["send"], FAR + 0.01) if late else begin + SHIFT["send"]
        steps.append((when if k else -100.0, k, "send"))
        clock.append(now)
    hops = len(masks)
    for k, size in enumerate(sizes):
        steps.append((clock[k] + SHIFT["sum"], k, "sum"))
        _, now = send_over("pair", clock[k] + STEP, size / 2)
        for t in range(2, hops):
            steps.append((now + SHIFT["far"], k, ("far", t)))
            _, now = send_over(("far", t), now + STEP, size)
        steps.append((now + SHIFT["back"], k, "back"))
        _, now = send_over("pair back", now + STEP, size / 2)
        steps.append((now + SHIFT["join"], k, "join"))
        finals.append(now)
    for k, size in enumerate(sizes):
        _, now = send_over("x", finals[k] + STEP, size)
        arrivals.append(now)
    batches, ends = BATCHES, []
    for i, groups in enumerate(batches):
        needed = [k for k, runs in enumerate(pieces) if any(run[0] in groups for run in runs)]
        now = max((finals if aligned else arrivals)[k] for k in needed) + 0.01 + SHIFT["trail"]
        for t in range(len(spread) + 1):
            steps.append((now, i, ("trail", t)))
            ends.append(now)
            now += HOP + STEP + UNIT * len(groups) / (t + 1)
        steps.append((ends[-1] + 0.01, i, "factor"))
    for k, now in enumerate(arrivals):
        now = now + SHIFT["other"] if k < count - 1 or not aligned else min(now, ends[-1] + AHEAD)
        steps.append((now, k, "other"))
    steps.sort(key=lambda step: step[0])
    if share % LANES == 0 and row_count == 4:
        ids = jnp.stack([jnp.stack(share_order(r)), jnp.stack(share_order(source))])
        ids, ordered = ids.astype(jnp.int32), inverse
    else:
        ids = None
        ordered = take(take(inverse, share_order(r), 0), share_order(source), 1)
    factors = []

    state, mine, others = [None] * count, [None] * count, [None] * count
    trailing = [None] * len(batches)
    def scale(*positions):
        scaled.update(zip(positions, scaled_quarters(order, positions, border, after(weights))))
        done(*(scaled[position] for position in positions))

    scale(3)

    for _, k, name in steps:
        if name in ("send", "sum"):
            both = [scaled[2 * half + (name == "send")] for half in (0, 1)]
        if name == "kept":
            scale(0, 2)
            continue
        if name == "send" and k == 0:
            state[k] = over_scen(first_send, 1)
        elif name == "send":
            values = list(heads)
            for g in sorted({run[0] for run in pieces[k]}):
                values[g] = after(heads[g])
            send = piece_to_send(pieces[k], both, values)
            done(send)
            state[k] = over_scen(send, 1)
        elif name == "heads":
            far = list(after(*far)) if len(far) > 1 else [after(far[0])]
            done(*far)
            heads[2:] = joined(far), joined([over_row(value, 1) for value in far])
        elif name == "sum":
            keep, send = piece_sum(pieces[k], part, both, heads, after(state[k]))
            done(keep, send)
            state[k] = keep, over_scen(send, 2)
        elif name[0] == "far" or name == "back":
            total, got = after(*state[k])
            total = total + got.astype(f32)
            if name == "back":
                total = total.astype(bf16)
            done(total)
            state[k] = total, over_scen(total, 2 if name == "back" else masks[name[1]])
        elif name == "join":
            mine[k] = join_halves(part, *after(*state[k]))
            done(mine[k])
            others[k] = over_scen(mine[k], 1)
        elif name == "other":
            others[k] = after(others[k])
            done(others[k])
        elif name == "slab":
            held = held_slab(order, after(slab))
            done(held)
        elif name == "factor":
            rows = after(trailing[k])
            last_one = k == len(batches) - 1
            factors = [
                factor(ids, ordered, tuple(widths), [batches[k]], [rows], factors, bf16 if last_one else f32)
            ]
            done(*factors)
        else:
            t = name[1]
            if t == 0:
                rows = trailing_rows(batches[k])
            else:
                rows, got = after(*trailing[k])
                rows = rows + got
            done(rows)
            trailing[k] = rows
            if t < len(spread):
                trailing[k] = rows, lax.ppermute(rows, ("scen", "row"), spread[t])

    places = []
    for k in range(count):
        for g, h, begin, end, at_row in offsets[k]:
            places.append((g, 0, h, begin, end, k, at_row))
            places.append((g, 1, h, begin, end, count + k, at_row))
    return update(order, held, factors[0], (tuple(widths), places), mine + others)


def solution(mesh):
    return jax.shard_map(
        body,
        mesh=mesh,
        in_specs=(P("scen", "row", None), P("scen", None), P(), P(), P(), P("row", "scen")),
        out_specs=P("row", "scen"),
        check_vma=False,
    )
```

```python
import functools

import jax
import jax.numpy as jnp
from jax import lax
from jax.experimental import pallas as pl
from jax.experimental.pallas import tpu as pltpu
from jax.sharding import PartitionSpec as P

f32, bf16 = jnp.float32, jnp.bfloat16
LANES = 128
MIB = 1 << 20
LIMIT, LIMIT_FIRST, LIMIT_REST = 10 * MIB, 54 * MIB, 50 * MIB
SEND_US, SUM_US, JOIN_US, REST_US, TAIL_US = 2.00, 0.54, 1.00, 26.64, 0.92
IN_VMEM = pl.BlockSpec(memory_space=pltpu.VMEM)
IN_HBM = pl.BlockSpec(memory_space=pltpu.HBM)
PIECES = ((2, 3, 3), (4, 4))
UNIT, HOP, STEP, FAR, SLAB, AHEAD = 2.85, 2.00, 1.50, 17.72, 83.09, 99.00
KEPT = 6.00
SHIFT = {'send': -1.5, 'sum': 1.32, 'far': 0.0, 'back': 0.0, 'join': 0.0, 'other': 0.0, 'trail': 0.0}
BATCHES = ((0, 1, 2), (3,))


def cost(us):
    return pl.CostEstimate(flops=int(us * 1e9), bytes_accessed=int(us * 2e6), transcendentals=0)


def nt_dot(a, b):
    return lax.dot_general(a, b, (((1,), (1,)), ((), ())), preferred_element_type=f32)


def scaled_flat(blocks, weights):
    parts = [
        (blocks[k].astype(f32) * weights[k : k + 1, :]).astype(bf16) for k in range(blocks.shape[0])
    ]
    return jnp.concatenate(parts, axis=1)


def first_kernel(
    parts, place_ref, counts_ref, order_ref, index_ref, table_ref, border_ref, *rest
):
    weights_ref, heads_ref, scaled_ref, send_ref, held_heads, held, sems = rest
    slots, quarter, width = held.shape
    share = heads_ref.shape[0]
    step = slots // parts
    first = pl.multiple_of(order_ref[1] * quarter, quarter)
    near = pltpu.make_async_copy(border_ref.at[:, pl.ds(0, share), :], held_heads, sems.at[parts])
    near.start()
    copies = [
        pltpu.make_async_copy(
            border_ref.at[pl.ds(i * step, step), pl.ds(first, quarter), :],
            held.at[pl.ds(i * step, step)],
            sems.at[i],
        )
        for i in range(parts)
    ]
    for copy in copies:
        copy.start()

    index = index_ref[...]
    high, low = index // LANES, index % LANES
    total = jnp.zeros(index.shape, f32)
    for row in range(table_ref.shape[0]):
        entries = jnp.broadcast_to(table_ref[row : row + 1, :], index.shape)
        picked = jnp.take_along_axis(entries, low, axis=1, mode="promise_in_bounds")
        total = jnp.where(high == row, picked, total)
    live = lax.broadcasted_iota(jnp.int32, index.shape, 0) < counts_ref[place_ref[0]]
    weights_ref[...] = jnp.where(live, total, 0.0)

    near.wait()
    heads_ref[...] = scaled_flat(held_heads, weights_ref[...])
    for i, copy in enumerate(copies):
        copy.wait()
        scaled_ref[:, i * step * width : (i + 1) * step * width] = scaled_flat(
            held.at[pl.ds(i * step, step)], weights_ref[i * step : (i + 1) * step, :]
        )
    send_ref[...] = nt_dot(scaled_ref[...], heads_ref[...]).astype(bf16)


def first_step(place, counts, order, col_index, barrier, border, share):
    slots, rows, width = border.shape
    quarter = rows // 4
    parts = 4 if slots % 4 == 0 else 1
    smem = pl.BlockSpec(memory_space=pltpu.SMEM)
    whole = lambda shape: pl.BlockSpec(shape, lambda i: (0,) * len(shape))
    table = barrier.reshape(-1, LANES)
    shapes = [
        jax.ShapeDtypeStruct(col_index.shape, f32),
        jax.ShapeDtypeStruct((share, slots * width), bf16),
        jax.ShapeDtypeStruct((quarter, slots * width), bf16),
        jax.ShapeDtypeStruct((quarter, share), bf16),
    ]
    return pl.pallas_call(
        functools.partial(first_kernel, parts),
        grid=(1,),
        in_specs=[smem, smem, smem, whole(col_index.shape), whole(table.shape), IN_HBM],
        out_specs=[whole(out.shape) for out in shapes],
        out_shape=shapes,
        scratch_shapes=[
            pltpu.VMEM((slots, share, width), bf16),
            pltpu.VMEM((slots, quarter, width), bf16),
            pltpu.SemaphoreType.DMA((parts + 1,)),
        ],
        cost_estimate=cost(REST_US),
        compiler_params=pltpu.CompilerParams(vmem_limit_bytes=LIMIT_FIRST),
        name="first_step",
    )(place, counts, order, col_index, table, border)


def scale_kernel(positions, parts, order_ref, border_ref, weights_ref, *rest):
    outs, held, sems = rest[: len(positions)], rest[-2], rest[-1]
    slots, rows, width = held.shape[1:]
    step = slots // parts
    copies = []
    for n, position in enumerate(positions):
        first = pl.multiple_of(order_ref[position] * rows, rows)
        copies += [
            pltpu.make_async_copy(
                border_ref.at[pl.ds(i * step, step), pl.ds(first, rows), :],
                held.at[n, pl.ds(i * step, step)],
                sems.at[n * parts + i],
            )
            for i in range(parts)
        ]
    for copy in copies:
        copy.start()
    for n, out in enumerate(outs):
        for i in range(parts):
            copies[n * parts + i].wait()
            out[:, i * step * width : (i + 1) * step * width] = scaled_flat(
                held.at[n, pl.ds(i * step, step)], weights_ref[i * step : (i + 1) * step, :]
            )


def scaled_quarters(order, positions, border, weights):
    slots, rows, width = border.shape
    quarter = rows // 4
    parts = 4 if slots % 4 == 0 else 1
    count = len(positions)
    return pl.pallas_call(
        functools.partial(scale_kernel, positions, parts),
        in_specs=[pl.BlockSpec(memory_space=pltpu.SMEM), IN_HBM, IN_VMEM],
        out_specs=[IN_VMEM] * count,
        out_shape=[jax.ShapeDtypeStruct((quarter, slots * width), bf16)] * count,
        scratch_shapes=[
            pltpu.VMEM((count, slots, quarter, width), bf16),
            pltpu.SemaphoreType.DMA((count * parts,)),
        ],
        cost_estimate=cost(REST_US),
        compiler_params=pltpu.CompilerParams(vmem_limit_bytes=LIMIT_REST),
        name="scaled_quarters",
    )(order, border, weights)


def piece_rows(runs, rows_refs, heads_refs, got, store):
    groups = sorted({g for g, _, _, _ in runs})
    at = 0
    for g, half, begin, end in runs:
        value = nt_dot(rows_refs[half][begin:end, :], heads_refs[groups.index(g)][...])
        place = slice(at, at + end - begin)
        if got is not None:
            value += got[place, :].astype(f32)
        store[place, :] = value.astype(store.dtype)
        at += end - begin


def send_kernel(runs, *refs):
    piece_rows(runs, refs[:2], refs[2:-1], None, refs[-1])


def sum_kernel(runs, part_ref, *refs):
    *heads, got, keep_ref, send_ref, total = refs[2:]
    piece_rows(runs, refs[:2], heads, got, total)
    half = keep_ref.shape[0]
    part = part_ref[0]
    keep_ref[...] = total[pl.ds(pl.multiple_of(part * half, half), half), :]
    send_ref[...] = total[pl.ds(pl.multiple_of((1 - part) * half, half), half), :].astype(bf16)


def piece_shape(runs, heads):
    groups = sorted({g for g, _, _, _ in runs})
    rows = sum(end - begin for _, _, begin, end in runs)
    return [heads[g] for g in groups], rows, heads[groups[0]].shape[0]


def piece_to_send(runs, scaled, heads):
    used, rows, columns = piece_shape(runs, heads)
    return pl.pallas_call(
        functools.partial(send_kernel, runs),
        in_specs=[IN_VMEM] * (2 + len(used)),
        out_specs=IN_VMEM,
        out_shape=jax.ShapeDtypeStruct((rows, columns), bf16),
        cost_estimate=cost(SEND_US),
        compiler_params=pltpu.CompilerParams(vmem_limit_bytes=LIMIT),
        name="piece_to_send",
    )(*scaled, *used)


def piece_sum(runs, part, scaled, heads, got):
    used, rows, columns = piece_shape(runs, heads)
    return pl.pallas_call(
        functools.partial(sum_kernel, runs),
        in_specs=[pl.BlockSpec(memory_space=pltpu.SMEM)] + [IN_VMEM] * (3 + len(used)),
        out_specs=[IN_VMEM] * 2,
        out_shape=[jax.ShapeDtypeStruct((rows // 2, columns), kind) for kind in (f32, bf16)],
        scratch_shapes=[pltpu.VMEM((rows, columns), f32)],
        cost_estimate=cost(SUM_US),
        compiler_params=pltpu.CompilerParams(vmem_limit_bytes=LIMIT),
        name="piece_sum",
    )(part, *scaled, *used, got)


def join_kernel(part_ref, own_ref, got_ref, out_ref):
    half = own_ref.shape[0]
    part = part_ref[0]
    out_ref[pl.ds(pl.multiple_of(part * half, half), half), :] = own_ref[...]
    out_ref[pl.ds(pl.multiple_of((1 - part) * half, half), half), :] = got_ref[...]


def join_halves(part, own, got):
    rows, columns = own.shape
    return pl.pallas_call(
        join_kernel,
        in_specs=[pl.BlockSpec(memory_space=pltpu.SMEM), IN_VMEM, IN_VMEM],
        out_specs=IN_VMEM,
        out_shape=jax.ShapeDtypeStruct((2 * rows, columns), own.dtype),
        cost_estimate=cost(JOIN_US),
        compiler_params=pltpu.CompilerParams(vmem_limit_bytes=LIMIT),
        name="join_halves",
    )(part, own, got)


def hold_kernel(order_ref, slab_ref, out_ref, sems):
    quarter = out_ref.shape[1]
    copies = []
    for p in range(4):
        rows = pl.ds(pl.multiple_of(order_ref[p] * quarter, quarter), quarter)
        copies.append(pltpu.make_async_copy(slab_ref.at[rows], out_ref.at[p], sems.at[p]))
    for copy in copies:
        copy.start()
    for copy in copies:
        copy.wait()


def held_slab(order, slab):
    rows, columns = slab.shape
    return pl.pallas_call(
        hold_kernel,
        in_specs=[pl.BlockSpec(memory_space=pltpu.SMEM), IN_HBM],
        out_specs=IN_VMEM,
        out_shape=jax.ShapeDtypeStruct((4, rows // 4, columns), slab.dtype),
        scratch_shapes=[pltpu.SemaphoreType.DMA((4,))],
        cost_estimate=cost(REST_US),
        compiler_params=pltpu.CompilerParams(vmem_limit_bytes=LIMIT),
        name="held_slab",
    )(order, slab)


def factor_kernel(plan, ids_ref, inverse_ref, *rest):
    widths, sources = plan
    n = len(widths)
    trailing, rest = rest[: len(sources)], rest[len(sources) :]
    total_ref, out_ref = rest if len(rest) == 2 else (None, rest[0])
    ends = [sum(widths[:g]) for g in range(n + 1)]
    begin_of = lambda which, g: (
        ends[g] if ids_ref is None else pl.multiple_of(ids_ref[which, g] * widths[g], widths[g])
    )
    for g in range(n):
        total = None if total_ref is None else total_ref[ends[g] : ends[g + 1], :]
        for batch, groups in enumerate(sources):
            begin = 0
            for j in groups:
                block = inverse_ref[pl.ds(begin_of(0, g), widths[g]), pl.ds(begin_of(1, j), widths[j])]
                part = nt_dot(block, trailing[batch][:, begin : begin + widths[j]])
                total = part if total is None else total + part
                begin += widths[j]
        out_ref[ends[g] : ends[g + 1], :] = total.astype(out_ref.dtype)


def factor(ids, inverse, widths, sources, trailing, total, kind):
    smem = pl.BlockSpec(memory_space=pltpu.SMEM)

    def kernel(*refs):
        factor_kernel((widths, sources), *((None, *refs) if ids is None else refs))

    operands = ([] if ids is None else [ids]) + [inverse, *trailing, *total]
    return pl.pallas_call(
        kernel,
        in_specs=([] if ids is None else [smem]) + [IN_VMEM] * (1 + len(trailing) + len(total)),
        out_specs=IN_VMEM,
        out_shape=jax.ShapeDtypeStruct((inverse.shape[0], trailing[0].shape[0]), kind),
        cost_estimate=cost(TAIL_US),
        compiler_params=pltpu.CompilerParams(vmem_limit_bytes=LIMIT),
        name="factor",
    )(*operands)


def update_kernel(plan, order_ref, slab_ref, factor_ref, *rest):
    widths, places = plan
    *pieces, out_ref, held, sems = rest
    quarter = held.shape[1]
    ends = [sum(widths[:g]) for g in range(len(widths) + 1)]
    stores = []
    for p in range(4):
        rows = pl.ds(pl.multiple_of(order_ref[p] * quarter, quarter), quarter)
        stores.append(pltpu.make_async_copy(held.at[p], out_ref.at[rows], sems.at[p]))
    eighth = quarter // 2
    for p in range(4):
        for first in (0, eighth):
            parts = []
            for g in range(len(widths)):
                for group, side, half, begin, end, piece, at in places:
                    if group == g and 2 * half + side == p and begin <= first < end:
                        start = at + first - begin
                        parts.append(pieces[piece][start : start + eighth, :])
            rows = slice(first, first + eighth)
            if all(width % LANES == 0 for width in widths):
                held[p, rows, :] = slab_ref[p, rows, :] - jnp.dot(
                    jnp.concatenate(parts, axis=1), factor_ref[...], preferred_element_type=f32
                )
            else:
                held[p, rows, :] = slab_ref[p, rows, :]
                for g, part in enumerate(parts):
                    held[p, rows, :] -= jnp.dot(
                        part, factor_ref[ends[g] : ends[g + 1], :], preferred_element_type=f32
                    )
        stores[p].start()
    for store in stores:
        store.wait()


def update(order, held, factor_value, plan, pieces):
    _, quarter, columns = held.shape
    return pl.pallas_call(
        functools.partial(update_kernel, plan),
        in_specs=[pl.BlockSpec(memory_space=pltpu.SMEM)] + [IN_VMEM] * (2 + len(pieces)),
        out_specs=IN_HBM,
        out_shape=jax.ShapeDtypeStruct((4 * quarter, columns), held.dtype),
        scratch_shapes=[
            pltpu.VMEM(held.shape, f32),
            pltpu.SemaphoreType.DMA((4,)),
        ],
        cost_estimate=cost(TAIL_US),
        compiler_params=pltpu.CompilerParams(vmem_limit_bytes=LIMIT),
        name="update",
    )(order, held, factor_value, *pieces)


def body(border, col_index, barrier, counts, inverse, slab):
    scen_count, row_count = lax.axis_size("scen"), lax.axis_size("row")
    s, r = lax.axis_index("scen"), lax.axis_index("row")
    slots, local_rows, width = border.shape
    panel_width = inverse.shape[0]
    share = panel_width // row_count
    quarter = local_rows // 4
    trail = slab.shape[1]
    x, z = s % 2, s // 2
    order = jnp.stack([x, 1 - x, 2 + x, 3 - x]).astype(jnp.int32)

    masks = [1 << bit for bit in range((scen_count - 1).bit_length())]
    part = (z % 2).astype(jnp.int32).reshape(1)
    over_scen = lambda value, mask: lax.ppermute(
        value.astype(bf16), "scen", [(i, i ^ mask) for i in range(scen_count)]
    )
    over_row = lambda value, mask: lax.ppermute(
        value, "row", [(i, i ^ mask) for i in range(row_count)]
    )

    last = []

    def after(*values):
        if not last:
            return values if len(values) > 1 else values[0]
        out = lax.optimization_barrier((*values, *last))
        return out[: len(values)] if len(values) > 1 else out[0]

    def done(*values):
        last[:] = values

    place = s.astype(jnp.int32).reshape(1)
    weights, own, scaled_sent, first_send = first_step(
        place, counts, order, col_index, barrier, border, share
    )
    scaled = {1: scaled_sent}
    done(own)
    far = [over_row(own, mask) for mask in range(2, row_count, 2)]
    sibling = over_row(own, 1)
    joined = lambda group: group[0] if len(group) == 1 else jnp.concatenate(group, axis=0)
    heads = [own, sibling, None, None]
    widths = [share, share, share * len(far), share * len(far)]

    def share_order(device):
        masks = [0, 1] + list(range(2, row_count, 2)) + list(range(3, row_count, 2))
        return [device ^ mask for mask in masks]

    first_row = s * trail
    source = first_row // local_rows

    def take(value, shares, axis):
        return jnp.concatenate(
            [lax.dynamic_slice_in_dim(value, k * share, share, axis) for k in shares], axis
        )

    aligned = trail <= quarter and all(
        (g * trail) % local_rows // quarter % 2 == g % 2 for g in range(scen_count)
    )
    unit = min(trail, quarter)
    row_masks = [1 << k for k in reversed(range((row_count - 1).bit_length()))]
    spread = []
    reached = {g: {g * trail // local_rows} for g in range(scen_count)}
    for mask in row_masks:
        spread.append(
            [
                (g * row_count + k, g * row_count + (k ^ mask))
                for g in range(scen_count)
                for k in sorted(reached[g])
            ]
        )
        for g in range(scen_count):
            reached[g] |= {k ^ mask for k in reached[g]}

    eighth = quarter // 2
    pieces = []
    for pair, sizes in enumerate(PIECES):
        units = [(2 * pair + g, b // 2, b % 2) for g in range(2) for b in range(4)]
        for size in sizes:
            runs = []
            for g, half, spot in units[:size]:
                if runs and runs[-1][:2] == (g, half):
                    runs[-1] = (*runs[-1][:3], (spot + 1) * eighth)
                else:
                    runs.append((g, half, spot * eighth, (spot + 1) * eighth))
            pieces.append(runs)
            units = units[size:]
    sizes = [size for pair in PIECES for size in pair]
    count = len(pieces)
    offsets = []
    for runs in pieces:
        places, at_row = [], 0
        for g, h, begin, end in runs:
            places.append((g, h, begin, end, at_row))
            at_row += end - begin
        offsets.append(places)
    last_of = [max(k for k, runs in enumerate(pieces) if any(run[0] == g for run in runs)) for g in range(4)]

    def kept_rows(values, g):
        parts = []
        for k, places in enumerate(offsets):
            parts += [values[k][at : at + end - begin] for h, _, begin, end, at in places if h == g]
        return jnp.concatenate(parts, axis=0)

    def trailing_rows(groups):
        columns = []
        for g in groups:
            kept, parts = kept_rows(mine, g), []
            other = None if aligned else kept_rows(others, g)
            for i in range(trail // unit):
                start = first_row % local_rows + i * unit
                place, inside = start // quarter, start % quarter
                begin = place // 2 * quarter + inside
                value = lax.dynamic_slice_in_dim(kept, begin, unit, 0)
                if not aligned:
                    value = jnp.where(
                        place % 2 == x, value, lax.dynamic_slice_in_dim(other, begin, unit, 0)
                    )
                parts.append(value)
            columns.append(parts[0] if len(parts) == 1 else jnp.concatenate(parts, axis=0))
        rows = columns[0] if len(columns) == 1 else jnp.concatenate(columns, axis=1)
        return jnp.where(source == r, rows, jnp.zeros_like(rows))

    steps, free = [(FAR, 0, "heads"), (SLAB, 0, "slab"), (KEPT, 0, "kept")], {}

    def send_over(link, ready, size):
        begin = max(ready, free.get(link, 0.0))
        free[link] = begin + size * UNIT
        return begin, free[link] + HOP

    clock, finals, arrivals = [], [], []
    for k, size in enumerate(sizes):
        begin, now = send_over("x", 0.0, size)
        late = any(run[0] >= 2 for run in pieces[k])
        when = max(begin + SHIFT["send"], FAR + 0.01) if late else begin + SHIFT["send"]
        steps.append((when if k else -100.0, k, "send"))
        clock.append(now)
    hops = len(masks)
    for k, size in enumerate(sizes):
        steps.append((clock[k] + SHIFT["sum"], k, "sum"))
        _, now = send_over("pair", clock[k] + STEP, size / 2)
        for t in range(2, hops):
            steps.append((now + SHIFT["far"], k, ("far", t)))
            _, now = send_over(("far", t), now + STEP, size)
        steps.append((now + SHIFT["back"], k, "back"))
        _, now = send_over("pair back", now + STEP, size / 2)
        steps.append((now + SHIFT["join"], k, "join"))
        finals.append(now)
    for k, size in enumerate(sizes):
        _, now = send_over("x", finals[k] + STEP, size)
        arrivals.append(now)
    batches, ends = BATCHES, []
    for i, groups in enumerate(batches):
        needed = [k for k, runs in enumerate(pieces) if any(run[0] in groups for run in runs)]
        now = max((finals if aligned else arrivals)[k] for k in needed) + 0.01 + SHIFT["trail"]
        for t in range(len(spread) + 1):
            steps.append((now, i, ("trail", t)))
            ends.append(now)
            now += HOP + STEP + UNIT * len(groups) / (t + 1)
        steps.append((ends[-1] + 0.01, i, "factor"))
    for k, now in enumerate(arrivals):
        now = now + SHIFT["other"] if k < count - 1 or not aligned else min(now, ends[-1] + AHEAD)
        steps.append((now, k, "other"))
    steps.sort(key=lambda step: step[0])
    if share % LANES == 0 and row_count == 4:
        ids = jnp.stack([jnp.stack(share_order(r)), jnp.stack(share_order(source))])
        ids, ordered = ids.astype(jnp.int32), inverse
    else:
        ids = None
        ordered = take(take(inverse, share_order(r), 0), share_order(source), 1)
    factors = []

    state, mine, others = [None] * count, [None] * count, [None] * count
    trailing = [None] * len(batches)
    def scale(*positions):
        scaled.update(zip(positions, scaled_quarters(order, positions, border, after(weights))))
        done(*(scaled[position] for position in positions))

    scale(3)

    for _, k, name in steps:
        if name in ("send", "sum"):
            both = [scaled[2 * half + (name == "send")] for half in (0, 1)]
        if name == "kept":
            scale(0, 2)
            continue
        if name == "send" and k == 0:
            state[k] = over_scen(first_send, 1)
        elif name == "send":
            values = list(heads)
            for g in sorted({run[0] for run in pieces[k]}):
                values[g] = after(heads[g])
            send = piece_to_send(pieces[k], both, values)
            done(send)
            state[k] = over_scen(send, 1)
        elif name == "heads":
            far = list(after(*far)) if len(far) > 1 else [after(far[0])]
            done(*far)
            heads[2:] = joined(far), joined([over_row(value, 1) for value in far])
        elif name == "sum":
            keep, send = piece_sum(pieces[k], part, both, heads, after(state[k]))
            done(keep, send)
            state[k] = keep, over_scen(send, 2)
        elif name[0] == "far" or name == "back":
            total, got = after(*state[k])
            total = total + got.astype(f32)
            if name == "back":
                total = total.astype(bf16)
            done(total)
            state[k] = total, over_scen(total, 2 if name == "back" else masks[name[1]])
        elif name == "join":
            mine[k] = join_halves(part, *after(*state[k]))
            done(mine[k])
            others[k] = over_scen(mine[k], 1)
        elif name == "other":
            others[k] = after(others[k])
            done(others[k])
        elif name == "slab":
            held = held_slab(order, after(slab))
            done(held)
        elif name == "factor":
            rows = after(trailing[k])
            last_one = k == len(batches) - 1
            factors = [
                factor(ids, ordered, tuple(widths), [batches[k]], [rows], factors, bf16 if last_one else f32)
            ]
            done(*factors)
        else:
            t = name[1]
            if t == 0:
                rows = trailing_rows(batches[k])
            else:
                rows, got = after(*trailing[k])
                rows = rows + got
            done(rows)
            trailing[k] = rows
            if t < len(spread):
                trailing[k] = rows, lax.ppermute(rows, ("scen", "row"), spread[t])

    places = []
    for k in range(count):
        for g, h, begin, end, at_row in offsets[k]:
            places.append((g, 0, h, begin, end, k, at_row))
            places.append((g, 1, h, begin, end, count + k, at_row))
    return update(order, held, factors[0], (tuple(widths), places), mine + others)


def solution(mesh):
    return jax.shard_map(
        body,
        mesh=mesh,
        in_specs=(P("scen", "row", None), P("scen", None), P(), P(), P(), P("row", "scen")),
        out_specs=P("row", "scen"),
        check_vma=False,
    )
```
